128 devices in a mesh: grp: 8 (over z_lo, y), mem: 16 (over z_hi, x, core).
Axes of the slice: x: 4, y: 4, z: 4 (z_hi: 2, z_lo: 2; z = z_hi * 2 + z_lo), core: 2. Of those that a mesh axis runs over, the one named last changes fastest.
Arguments:
- fine_rows: bfloat16 [24576, 768], P(('grp', 'mem')), may hold values from -6 to 6
- coarse_rows: bfloat16 [24576, 768], P(('grp', 'mem')), may hold values from -6 to 6
- fine_head: bfloat16 [768, 768], replicated, may hold values from -0.0078125 to 0.0078125
- coarse_head: bfloat16 [768, 768], replicated, may hold values from -0.0078125 to 0.0078125
- log_scale: float32 [1], replicated, may hold values from 1.5 to 2.5
- bias: float32 [1], replicated, may hold values from -6 to -3
Outputs:
- loss: float32 [1], replicated
- fine_grad: float32 [24576, 768], P(('grp', 'mem'))
- coarse_grad: float32 [24576, 768], P(('grp', 'mem'))
- fine_head_grad: float32 [768, 768], replicated
- coarse_head_grad: float32 [768, 768], replicated
The draws below stay inside these ranges and needn't reach their ends.
All inputs are finite; a program needn't handle non-finite values.
Results may differ from the reference program's by a relative error of at most 0.02.
Values may be sent and summed in bfloat16 or wider, within the bound.
A program may use at most 128 MiB of HBM per device.

```python
import jax
import jax.numpy as jnp
from jax import lax

D = 768
ROWS_DEV = 192
TOKENS = 24576
N_MEM = 16


def shard_levels(own_key, extent, pieces, low, high):
    factor_of = 1.0
    for axis_at, parts in pieces:
        steps = jax.random.uniform(jax.random.fold_in(jax.random.fold_in(own_key, 6), axis_at), (parts,), jnp.float32, low / len(pieces), high / len(pieces))
        factor_of = factor_of * jnp.repeat(jnp.exp(steps), extent[axis_at] // parts).reshape((-1,) + (1,) * (len(extent) - 1 - axis_at))
    return factor_of


def centred(key, shape, spread, reach, cuts=(), held_as=jnp.bfloat16):
    loudness = shard_levels(key, shape, cuts, -0.22, 0.18) if cuts else 1.0
    values = jax.random.normal(key, shape, jnp.float32) * spread * loudness
    return jnp.minimum(jnp.maximum(values, -reach), reach).astype(held_as)


def setup_inputs(seed: int = 0) -> dict:
    streams_of = jax.random.split(jax.random.key(seed), 7)
    fine_rows = centred(streams_of[0], (TOKENS, D), 1.0, 6.0, ((0, 128),))
    coarse_rows = centred(streams_of[1], (TOKENS, D), 1.0, 6.0, ((0, 128),))
    fine_head = centred(streams_of[2], (D, D), (D * D) ** -0.5, 0.0078125)
    coarse_head = centred(streams_of[3], (D, D), (D * D) ** -0.5, 0.0078125)
    log_scale = jnp.clip(jax.random.uniform(streams_of[4], (1,), jnp.float32, 1.5, 2.5), 1.5, 2.5)
    bias = jnp.clip(jax.random.uniform(streams_of[5], (1,), jnp.float32, -6.0, -3.0), -6.0, -3.0)
    return {"fine_rows": fine_rows, "coarse_rows": coarse_rows, "fine_head": fine_head, "coarse_head": coarse_head, "log_scale": log_scale, "bias": bias}


EPS = 1e-06

def embed(rows, weight):
    proj = jnp.dot(rows, weight, preferred_element_type=jnp.float32)
    inv = lax.rsqrt(lax.optimization_barrier(jnp.sum(proj * proj, axis=-1, keepdims=True)) + EPS)
    return (proj * inv, inv)

def head_back(unit, inv, grad_unit):
    inner = lax.optimization_barrier(jnp.sum(unit * grad_unit, axis=-1, keepdims=True))
    return (inv * (grad_unit - unit * inner)).astype(jnp.bfloat16)

def reference(fine_rows, coarse_rows, fine_head, coarse_head, log_scale, bias):
    fine_unit, fine_inv = embed(fine_rows, fine_head)
    coarse_unit, coarse_inv = embed(coarse_rows, coarse_head)
    fine_emb = fine_unit.astype(jnp.bfloat16)
    coarse_emb = coarse_unit.astype(jnp.bfloat16)
    scale = jnp.exp(log_scale[0])
    shift = bias[0]
    block = ROWS_DEV * N_MEM
    count = TOKENS // block
    col_ids = jnp.arange(TOKENS, dtype=jnp.int32)

    def step(carry, index):
        acc_cols, total = carry
        start = index * block
        rows_block = lax.dynamic_slice_in_dim(fine_emb, start, block, 0)
        row_ids = start + jnp.arange(block, dtype=jnp.int32)
        sign = jnp.where(row_ids[:, None] == col_ids[None, :], 1.0, -1.0).astype(jnp.float32)
        logit = scale * lax.dot_general(rows_block, coarse_emb, (((1,), (1,)), ((), ())), preferred_element_type=jnp.float32) + shift
        margin = sign * logit
        total = total + jnp.sum(jax.nn.softplus(-margin))
        coef = (-sign * jax.nn.sigmoid(-margin) * scale).astype(jnp.bfloat16)
        grad_rows = jnp.dot(coef, coarse_emb, preferred_element_type=jnp.float32)
        acc_cols = acc_cols + lax.dot_general(coef, rows_block, (((0,), (0,)), ((), ())), preferred_element_type=jnp.float32)
        return ((acc_cols, total), grad_rows)
    init = (jnp.zeros((TOKENS, D), jnp.float32), jnp.zeros((), jnp.float32))
    (coarse_dz, total), blocks = lax.scan(step, init, jnp.arange(count, dtype=jnp.int32))
    fine_dz = blocks.reshape(TOKENS, D)
    fine_dp = head_back(fine_unit, fine_inv, fine_dz)
    coarse_dp = head_back(coarse_unit, coarse_inv, coarse_dz)
    dims = (((1,), (1,)), ((), ()))
    fine_grad = lax.dot_general(fine_dp, fine_head, dims, preferred_element_type=jnp.float32)
    coarse_grad = lax.dot_general(coarse_dp, coarse_head, dims, preferred_element_type=jnp.float32)
    outer = (((0,), (0,)), ((), ()))
    fine_head_grad = lax.dot_general(fine_rows, fine_dp, outer, preferred_element_type=jnp.float32)
    coarse_head_grad = lax.dot_general(coarse_rows, coarse_dp, outer, preferred_element_type=jnp.float32)
    loss = jnp.reshape(total / (TOKENS * TOKENS), (1,))
    return (loss, fine_grad, coarse_grad, fine_head_grad, coarse_head_grad)
```

```python
import jax
import jax.numpy as jnp
from jax import lax
from jax.experimental import pallas as pl
from jax.experimental.pallas import tpu as pltpu
from jax.sharding import PartitionSpec as P

MESH = pl.DeviceIdType.MESH
EPS = 1e-06
F32 = jnp.float32
BF16 = jnp.bfloat16
VMEM = pltpu.VMEM


def dot(a, b, dims):
    return lax.dot_general(a, b, (dims, ((), ())), preferred_element_type=F32)


NN = ((1,), (0,))
NT = ((1,), (1,))
TN = ((0,), (0,))


class Place:
    def __init__(self):
        grp, mem = lax.axis_index("grp"), lax.axis_index("mem")
        self.core = mem % 2
        self.x, self.y = (mem // 2) % 4, grp % 4
        self.z = (mem // 8) * 2 + grp // 4
        self.steps = {("x", d): self.at(dx=d) for d in (1, 2, 3)}
        self.steps |= {("y", d): self.at(dy=d) for d in (1, 2, 3)}
        self.steps |= {("z", d): self.at(z=(self.z + d) % 4) for d in (1, 2, 3)}
        self.sibling = self.at(core=1 - self.core)
        self.other_hi = self.steps["z", 2]
        self.other_lo = self.at(z=self.z + 1 - 2 * (self.z % 2))

    def at(self, dx=0, dy=0, z=None, core=None):
        x, y = (self.x + dx) % 4, (self.y + dy) % 4
        z = self.z if z is None else z
        core = self.core if core is None else core
        return ((z % 2) * 4 + y, (z // 2) * 8 + x * 2 + core)

    def along(self, axis, step):
        return self.steps[axis, step]


def view(ref, *index):
    return ref.at[index] if index else ref


class Copies:
    def __init__(self, send_sem, recv_sem):
        self.send_sem, self.recv_sem = send_sem, recv_sem
        self.made = {}

    def start(self, name, src, dst, device):
        index = len(self.made)
        assert name not in self.made and index < N_COPIES

        def make():
            return pltpu.make_async_remote_copy(
                src_ref=view(*src),
                dst_ref=view(*dst),
                send_sem=self.send_sem.at[index],
                recv_sem=self.recv_sem.at[index],
                device_id=device,
                device_id_type=MESH,
            )

        self.made[name] = make
        make().start()

    def wait(self, *names):
        for name in names:
            self.made[name]().wait_recv()

    def finish(self):
        for make in self.made.values():
            make().wait_send()


N_COPIES = 96


def kernel(
    fine_rows,
    coarse_rows,
    fine_head,
    coarse_head,
    log_scale,
    bias,
    loss_out,
    fine_grad,
    coarse_grad,
    fine_head_grad,
    coarse_head_grad,
    fine_all,
    coarse_all,
    fine_acc,
    coarse_acc,
    unit_keep,
    inv_keep,
    rows_sib,
    consts,
    loss_acc,
    sib_out,
    sib_in,
    half_out,
    half_in,
    full_out,
    full_in,
    hop_out,
    hop_in,
    own_sum,
    dp_keep,
    dp_sib,
    part,
    part_out,
    part_in,
    quarter,
    quarter_out,
    quarter_in,
    column,
    whole,
    whole_sib,
    loss_parts,
    send_sem,
    recv_sem,
):
    rows, width = fine_rows.shape
    half = rows // 2
    wide = width // 2
    here = Place()
    copies = Copies(send_sem, recv_sem)
    upper, lower = pl.ds(0, half), pl.ds(half, half)

    def slot(step):
        return pl.ds((step % 4) * rows, rows)

    barrier = pltpu.get_barrier_semaphore()
    partners = [here.sibling]
    partners += [here.along(axis, step) for axis in "xyz" for step in (1, 2, 3)]
    for device in partners:
        pl.semaphore_signal(barrier, inc=1, device_id=device, device_id_type=MESH)

    consts[0] = 0.5 * jnp.exp(jnp.full((8, width), log_scale[0], F32))
    consts[1] = jnp.full((8, width), 0.5 * bias[0], F32)
    h, shift = consts[0, 0:1, :], consts[1, 0:1, :]

    def embed(which, rows_ref, head_ref):
        proj = dot(rows_ref[...], head_ref[...], NN)
        inv = lax.rsqrt(jnp.sum(proj * proj, axis=-1, keepdims=True) + EPS)
        unit = proj * inv
        unit_keep[which] = unit
        inv_keep[which] = inv
        return unit.astype(BF16)

    fine_all[0, slot(0)] = embed(0, fine_rows, fine_head)
    pl.semaphore_wait(barrier, len(partners))
    mine = (fine_all, 0, slot(0))
    copies.start("fz", mine, (fine_all, 2, slot(0)), here.other_hi)
    copies.start("fx+", mine, (fine_all, 0, slot(-1)), here.along("x", 1))
    copies.start("fx-", mine, (fine_all, 0, slot(1)), here.along("x", 3))
    copies.start("fs", mine, (fine_all, 1, slot(0)), here.sibling)

    coarse_all[0, slot(0)] = embed(1, coarse_rows, coarse_head)
    mine = (coarse_all, 0, slot(0))
    copies.start("cz", mine, (coarse_all, 1, slot(0)), here.other_lo)
    copies.start("cy+", mine, (coarse_all, 0, slot(-1)), here.along("y", 1))
    copies.start("cy-", mine, (coarse_all, 0, slot(1)), here.along("y", 3))
    copies.start("rf", (fine_rows,), (rows_sib, 0), here.sibling)
    copies.start("rc", (coarse_rows,), (rows_sib, 1), here.sibling)

    def pass_on(tag, axis, buf, at, sib_at):
        copies.wait(tag + "+")
        copies.start(tag + "++", (buf, at, pl.ds(3 * rows, half)), (buf, at, pl.ds(2 * rows, half)), here.along(axis, 1))
        if sib_at is not None:
            copies.start(tag + "+s", (buf, at, slot(-1)), (buf, sib_at, slot(-1)), here.sibling)
        copies.wait(tag + "-")
        copies.start(tag + "--", (buf, at, pl.ds(rows + half, half)), (buf, at, pl.ds(2 * rows + half, half)), here.along(axis, 3))
        if sib_at is not None:
            copies.start(tag + "-s", (buf, at, slot(1)), (buf, sib_at, slot(1)), here.sibling)

    def hand_over(tag, buf, at, sib_at):
        copies.wait(tag + "++", tag + "--")
        if sib_at is not None:
            copies.start(tag + "2s", (buf, at, slot(2)), (buf, sib_at, slot(2)), here.sibling)

    fine_acc[...] = jnp.zeros_like(fine_acc)
    coarse_acc[...] = jnp.zeros_like(coarse_acc)
    loss_acc[...] = jnp.zeros_like(loss_acc)

    fine_emb = fine_all[0, slot(0)].astype(F32)
    coarse_emb = coarse_all[0, slot(0)].astype(F32)
    arg = jnp.sum(fine_emb * coarse_emb, axis=-1, keepdims=True) * consts[0, 0:1, 0:1] + consts[1, 0:1, 0:1]
    tanh = jnp.tanh(arg)
    delta = (tanh - 1.0).astype(BF16).astype(F32) - (1.0 + tanh).astype(BF16).astype(F32)
    own_sum[0] = delta * coarse_emb
    own_sum[1] = delta * fine_emb
    diagonal = jnp.sum(2.0 * arg, axis=0, keepdims=True)

    pass_on("fx", "x", fine_all, 0, 1)
    pass_on("cy", "y", coarse_all, 0, None)
    copies.wait("fz")
    mine = (fine_all, 2, slot(0))
    copies.start("gx+", mine, (fine_all, 2, slot(-1)), here.along("x", 1))
    copies.start("gx-", mine, (fine_all, 2, slot(1)), here.along("x", 3))
    copies.start("gs", mine, (fine_all, 3, slot(0)), here.sibling)
    copies.wait("cz")
    mine = (coarse_all, 1, slot(0))
    copies.start("dy+", mine, (coarse_all, 1, slot(-1)), here.along("y", 1))
    copies.start("dy-", mine, (coarse_all, 1, slot(1)), here.along("y", 3))
    hand_over("fx", fine_all, 0, 1)
    hand_over("cy", coarse_all, 0, None)

    def tile(fg, cg):
        cols = coarse_all[cg]
        n = 256
        coefs = []
        for j in range(4 * rows // n):
            at = pl.ds(j * n, n)
            t = jnp.tanh(dot(fine_all[fg, at], cols, NT) * h + shift)
            coef = (1.0 + t).astype(BF16)
            rest = 1.0 - t
            eighth = n // 8
            p = [rest[i * eighth : (i + 1) * eighth] for i in range(8)]
            p = ((p[0] * p[1]) * (p[2] * p[3])) * ((p[4] * p[5]) * (p[6] * p[7]))
            p = jnp.log(p * (1.0 / 256.0))
            loss_acc[...] -= (p[0:8] + p[8:16]) + (p[16:24] + p[24:32])
            fine_acc[fg, at] += dot(coef, cols, NN)
            coefs.append(coef)
        coarse_acc[cg] += dot(jnp.concatenate(coefs, 0), fine_all[fg], TN)

    def to_sibling(k):
        sib_out[k] = fine_acc[2 * k + 1].astype(BF16)
        copies.start(f"sum_s{k}", (sib_out, k), (sib_in, k), here.sibling)

    def ring_start(tag, axis, r, acc, other):
        def total(step):
            value = acc[slot(step)]
            return value if other is None else value + other[slot(step)].astype(F32)

        half_out[r] = total(2).astype(BF16)
        copies.start(tag + "h+", (half_out, r, upper), (half_in, r, upper), here.along(axis, 1))
        copies.start(tag + "h-", (half_out, r, lower), (half_in, r, lower), here.along(axis, 3))
        if other is not None:
            for step in (0, 1, 3):
                acc[slot(step)] = total(step)

    def ring_middle(tag, axis, r, acc):
        copies.wait(tag + "h+")
        full_out[r, 0, upper] = (acc[pl.ds(rows, half)] + half_in[r, upper].astype(F32)).astype(BF16)
        full_out[r, 0, lower] = acc[pl.ds(rows + half, half)].astype(BF16)
        copies.start(tag + "f+", (full_out, r, 0), (full_in, r, 0), here.along(axis, 1))
        copies.wait(tag + "h-")
        full_out[r, 1, upper] = acc[pl.ds(3 * rows, half)].astype(BF16)
        full_out[r, 1, lower] = (acc[pl.ds(3 * rows + half, half)] + half_in[r, lower].astype(F32)).astype(BF16)
        copies.start(tag + "f-", (full_out, r, 1), (full_in, r, 1), here.along(axis, 3))

    def ring_end(tag, r, acc):
        copies.wait(tag + "f+", tag + "f-")
        return acc[slot(0)] + full_in[r, 0].astype(F32) + full_in[r, 1].astype(F32)

    def hop(tag, which, value, device):
        hop_out[which] = value.astype(BF16)
        copies.start(tag, (hop_out, which), (hop_in, which), device)

    def step(t, carry):
        @pl.when(t == 1)
        def _():
            copies.wait("fs", "fx+s", "fx-s", "fx2s")

        @pl.when(t == 2)
        def _():
            pass_on("gx", "x", fine_all, 2, 3)
            pass_on("dy", "y", coarse_all, 1, None)
            hand_over("gx", fine_all, 2, 3)

        @pl.when(t == 3)
        def _():
            copies.wait("gs", "gx+s", "gx-s", "gx2s")

        @pl.when(t == 4)
        def _():
            ring_start("c0", "y", 2, coarse_acc.at[0], None)
            hand_over("dy", coarse_all, 1, None)

        @pl.when(t == 5)
        def _():
            to_sibling(1)
            ring_middle("c0", "y", 2, coarse_acc.at[0])

        @pl.when(t == 6)
        def _():
            copies.wait("sum_s1")
            ring_start("f1", "x", 1, fine_acc.at[2], sib_in.at[1])
            own_sum[1] += ring_end("c0", 2, coarse_acc.at[0])

        @pl.when(t == 7)
        def _():
            to_sibling(0)
            ring_middle("f1", "x", 1, fine_acc.at[2])

        late = t // 4
        tile(t + late * (7 - 2 * t), late)
        return carry

    lax.fori_loop(0, 8, step, 0)

    copies.wait("sum_s0")
    ring_start("f0", "x", 0, fine_acc.at[0], sib_in.at[0])
    ring_start("c1", "y", 3, coarse_acc.at[1], None)
    hop("fhop", 0, ring_end("f1", 1, fine_acc.at[2]), here.other_hi)

    loss = loss_acc[:, 0:128]
    for i in range(1, width // 128):
        loss = loss + loss_acc[:, i * 128 : (i + 1) * 128]
    at_origin = (lax.broadcasted_iota(jnp.int32, (8, 128), 0) + lax.broadcasted_iota(jnp.int32, (8, 128), 1)) == 0
    loss = loss - jnp.where(at_origin, diagonal, 0.0)
    loss_parts[0, 0] = loss
    copies.start("loss_s", (loss_parts, 0, 0), (loss_parts, 0, 1), here.sibling)

    def loss_round(r, axis, place):
        if r == 1:
            copies.wait("loss_s")
            value = loss_parts[0, 0] + loss_parts[0, 1]
        else:
            copies.wait(*[f"loss{r - 1}{d}" for d in (1, 2, 3)])
            q = loss_parts
            value = (q[r - 1, 0] + q[r - 1, 1]) + (q[r - 1, 2] + q[r - 1, 3])
        if axis is None:
            return value
        loss_parts[r, place] = value
        for d in (1, 2, 3):
            copies.start(f"loss{r}{d}", (loss_parts, r, place), (loss_parts, r, place), here.along(axis, d))

    ring_middle("f0", "x", 0, fine_acc.at[0])
    ring_middle("c1", "y", 3, coarse_acc.at[1])
    loss_round(1, "x", here.x)

    def head_back(which, value):
        unit, inv = unit_keep[which], inv_keep[which]
        grad = value * h
        inner = jnp.sum(unit * grad, axis=-1, keepdims=True)
        dp = (inv * (grad - unit * inner)).astype(BF16)
        dp_keep[which, 0] = dp[:, 0:wide]
        dp_keep[which, 1] = dp[:, wide:]
        copies.start(f"dp{which}", (dp_keep, which, 1 - here.core), (dp_sib, which), here.sibling)

    def rows_grad(which, head_ref, out):
        head = head_ref[...]
        out[...] = dot(dp_keep[which, 0], head[:, 0:wide], NT) + dot(dp_keep[which, 1], head[:, wide:], NT)

    axes = {0: ("x", here.x, "y", here.y), 1: ("y", here.y, "x", here.x)}

    def head_part(which, rows_ref):
        first, at, _, _ = axes[which]
        copies.wait(f"dp{which}")
        value = dot(rows_ref[...], dp_keep[which, here.core], TN)
        value = value + dot(rows_sib[which], dp_sib[which], TN)
        for j in range(4):
            part[which, j] = value[j * rows : (j + 1) * rows]
            part_out[which, j] = value[j * rows : (j + 1) * rows].astype(BF16)
        for d in (1, 3, 2):
            copies.start(f"part{which}{d}", (part_out, which, (at + d) % 4), (part_in, which, d - 1), here.along(first, d))

    def head_quarter(which):
        _, at, second, place = axes[which]
        copies.wait(*[f"part{which}{d}" for d in (1, 2, 3)])
        value = part[which, at]
        for d in range(3):
            value = value + part_in[which, d].astype(F32)
        n = rows // 4
        for j in range(4):
            quarter[which, j] = value[j * n : (j + 1) * n]
            quarter_out[which, j] = value[j * n : (j + 1) * n].astype(BF16)
        for d in (1, 3, 2):
            copies.start(f"quarter{which}{d}", (quarter_out, which, (place + d) % 4), (quarter_in, which, d - 1), here.along(second, d))

    def head_column(which):
        _, _, _, place = axes[which]
        copies.wait(*[f"quarter{which}{d}" for d in (1, 2, 3)])
        value = quarter[which, place]
        for d in range(3):
            value = value + quarter_in[which, d].astype(F32)
        column[which, here.z] = value.astype(BF16)
        mine = (column, which, here.z)
        for d in (1, 3, 2):
            copies.start(f"column{which}{d}", mine, mine, here.along("z", d))

    def head_total(which):
        _, at, second, place = axes[which]
        copies.wait(*[f"column{which}{d}" for d in (1, 2, 3)])
        value = column[which, 0].astype(F32)
        for z in range(1, 4):
            value = value + column[which, z].astype(F32)
        whole[which, at, place] = value.astype(BF16)
        mine = (whole, which, at, place)
        for d in (1, 3, 2):
            copies.start(f"back{which}{d}", mine, mine, here.along(second, d))

    def head_spread(which):
        first, at, _, _ = axes[which]
        copies.wait(*[f"back{which}{d}" for d in (1, 2, 3)])
        mine = (whole, which, at)
        for d in (1, 3, 2):
            copies.start(f"spread{which}{d}", mine, mine, here.along(first, d))

    def head_share(which, out):
        copies.wait(*[f"spread{which}{d}" for d in (1, 2, 3)])
        copies.start(f"share{which}", (whole, which), (whole_sib, which), here.sibling)
        cols = pl.ds(pl.multiple_of(here.core * wide, 128), wide)
        n = rows // 4
        for i in range(4):
            for j in range(4):
                out[pl.ds(i * rows + j * n, n), cols] = whole[which, i, j].astype(F32)

    def head_write(which, out):
        copies.wait(f"share{which}")
        cols = pl.ds(pl.multiple_of((1 - here.core) * wide, 128), wide)
        n = rows // 4
        for i in range(4):
            for j in range(4):
                out[pl.ds(i * rows + j * n, n), cols] = whole_sib[which, i, j].astype(F32)

    value = ring_end("f0", 0, fine_acc.at[0]) + own_sum[0]
    copies.wait("fhop")
    head_back(0, value + hop_in[0].astype(F32))
    hop("chop", 1, ring_end("c1", 3, coarse_acc.at[1]), here.other_lo)
    copies.wait("rf", "rc")
    head_part(0, fine_rows)
    loss_round(2, "y", here.y)
    rows_grad(0, fine_head, fine_grad)
    copies.wait("chop")
    head_back(1, own_sum[1] + hop_in[1].astype(F32))
    head_part(1, coarse_rows)
    rows_grad(1, coarse_head, coarse_grad)
    loss_round(3, "z", here.z)
    head_quarter(0)
    head_quarter(1)
    head_column(0)
    head_column(1)
    head_total(0)
    head_total(1)
    head_spread(0)
    head_spread(1)
    total = loss_round(4, None, None)
    pairs = float(rows * 128) ** 2
    loss_out[0] = jnp.sum(total) * (1.0 / pairs)
    head_share(0, fine_head_grad)
    head_share(1, coarse_head_grad)
    head_write(0, fine_head_grad)
    head_write(1, coarse_head_grad)
    copies.finish()


def shards(fine_rows, coarse_rows, fine_head, coarse_head, log_scale, bias):
    rows, width = fine_rows.shape
    wide, n = width // 2, rows // 4
    vmem = pl.BlockSpec(memory_space=pltpu.VMEM)
    smem = pl.BlockSpec(memory_space=pltpu.SMEM)
    scratch = [
        VMEM((4, 4 * rows, width), BF16),
        VMEM((2, 4 * rows, width), BF16),
        VMEM((4, 4 * rows, width), F32),
        VMEM((2, 4 * rows, width), F32),
        VMEM((2, rows, width), F32),
        VMEM((2, rows, 1), F32),
        VMEM((2, rows, width), BF16),
        VMEM((2, 8, width), F32),
        VMEM((8, width), F32),
        VMEM((2, 4 * rows, width), BF16),
        VMEM((2, 4 * rows, width), BF16),
        VMEM((4, rows, width), BF16),
        VMEM((4, rows, width), BF16),
        VMEM((4, 2, rows, width), BF16),
        VMEM((4, 2, rows, width), BF16),
        VMEM((2, rows, width), BF16),
        VMEM((2, rows, width), BF16),
        VMEM((2, rows, width), F32),
        VMEM((2, 2, rows, wide), BF16),
        VMEM((2, rows, wide), BF16),
        VMEM((2, 4, rows, wide), F32),
        VMEM((2, 4, rows, wide), BF16),
        VMEM((2, 3, rows, wide), BF16),
        VMEM((2, 4, n, wide), F32),
        VMEM((2, 4, n, wide), BF16),
        VMEM((2, 3, n, wide), BF16),
        VMEM((2, 4, n, wide), BF16),
        VMEM((2, 4, 4, n, wide), BF16),
        VMEM((2, 4, 4, n, wide), BF16),
        VMEM((4, 4, 8, 128), F32),
        pltpu.SemaphoreType.DMA((N_COPIES,)),
        pltpu.SemaphoreType.DMA((N_COPIES,)),
    ]
    tokens = rows * lax.axis_size("grp") * lax.axis_size("mem")
    pair_flops = 6 * (16 * rows) * (8 * rows) * width
    return pl.pallas_call(
        kernel,
        out_shape=(
            jax.ShapeDtypeStruct((1,), F32),
            jax.ShapeDtypeStruct((rows, width), F32),
            jax.ShapeDtypeStruct((rows, width), F32),
            jax.ShapeDtypeStruct((width, width), F32),
            jax.ShapeDtypeStruct((width, width), F32),
        ),
        in_specs=[vmem, vmem, vmem, vmem, smem, smem],
        out_specs=(smem, vmem, vmem, vmem, vmem),
        scratch_shapes=scratch,
        cost_estimate=pl.CostEstimate(flops=pair_flops, bytes_accessed=tokens * width, transcendentals=0),
        compiler_params=pltpu.CompilerParams(collective_id=0, has_side_effects=True, vmem_limit_bytes=58 * 2**20),
    )(fine_rows, coarse_rows, fine_head, coarse_head, log_scale, bias)


def solution(mesh):
    placed = (P(("grp", "mem"), None), P(("grp", "mem"), None), P(), P(), P(), P())
    return jax.shard_map(
        shards,
        mesh=mesh,
        in_specs=placed,
        out_specs=(P(), P(("grp", "mem"), None), P(("grp", "mem"), None), P(), P()),
        check_vma=False,
    )
```

```python
import jax
import jax.numpy as jnp
from jax import lax
from jax.experimental import pallas as pl
from jax.experimental.pallas import tpu as pltpu
from jax.sharding import PartitionSpec as P

MESH = pl.DeviceIdType.MESH
EPS = 1e-06
F32 = jnp.float32
BF16 = jnp.bfloat16
VMEM = pltpu.VMEM


def dot(a, b, dims):
    return lax.dot_general(a, b, (dims, ((), ())), preferred_element_type=F32)


NN = ((1,), (0,))
NT = ((1,), (1,))
TN = ((0,), (0,))


class Place:
    def __init__(self):
        grp, mem = lax.axis_index("grp"), lax.axis_index("mem")
        self.core = mem % 2
        self.x, self.y = (mem // 2) % 4, grp % 4
        self.z = (mem // 8) * 2 + grp // 4
        self.steps = {("x", d): self.at(dx=d) for d in (1, 2, 3)}
        self.steps |= {("y", d): self.at(dy=d) for d in (1, 2, 3)}
        self.steps |= {("z", d): self.at(z=(self.z + d) % 4) for d in (1, 2, 3)}
        self.sibling = self.at(core=1 - self.core)
        self.other_hi = self.steps["z", 2]
        self.other_lo = self.at(z=self.z + 1 - 2 * (self.z % 2))

    def at(self, dx=0, dy=0, z=None, core=None):
        x, y = (self.x + dx) % 4, (self.y + dy) % 4
        z = self.z if z is None else z
        core = self.core if core is None else core
        return ((z % 2) * 4 + y, (z // 2) * 8 + x * 2 + core)

    def along(self, axis, step):
        return self.steps[axis, step]


def view(ref, *index):
    return ref.at[index] if index else ref


class Copies:
    def __init__(self, send_sem, recv_sem):
        self.send_sem, self.recv_sem = send_sem, recv_sem
        self.made = {}

    def start(self, name, src, dst, device):
        index = len(self.made)
        assert name not in self.made and index < N_COPIES

        def make():
            return pltpu.make_async_remote_copy(
                src_ref=view(*src),
                dst_ref=view(*dst),
                send_sem=self.send_sem.at[index],
                recv_sem=self.recv_sem.at[index],
                device_id=device,
                device_id_type=MESH,
            )

        self.made[name] = make
        make().start()

    def wait(self, *names):
        for name in names:
            self.made[name]().wait_recv()

    def finish(self):
        for make in self.made.values():
            make().wait_send()


N_COPIES = 128
ORDERS = (("x", "y", "z"), ("y", "z", "x"), ("z", "x", "y"))


def kernel(
    fine_rows,
    coarse_rows,
    fine_head,
    coarse_head,
    log_scale,
    bias,
    loss_out,
    fine_grad_out,
    coarse_grad_out,
    heads_out,
    fine_all,
    coarse_all,
    fine_acc,
    coarse_acc,
    unit_keep,
    inv_keep,
    rows_keep,
    consts,
    loss_acc,
    sib_out,
    sib_in,
    half_out,
    half_in,
    full_out,
    full_in,
    hop_out,
    hop_in,
    own_sum,
    dp_keep,
    grad_keep,
    part_out,
    part_in,
    quarter_out,
    quarter_in,
    column,
    heads,
    loss_parts,
    send_sem,
    recv_sem,
    local_sem,
):
    rows, width = fine_rows.shape
    half = rows // 2
    wide = width // 2
    here = Place()
    copies = Copies(send_sem, recv_sem)
    upper, lower = pl.ds(0, half), pl.ds(half, half)

    def slot(step):
        return pl.ds((step % 4) * rows, rows)

    def slot_half(step, which):
        return pl.ds((step % 4) * rows + which * half, half)

    barrier = pltpu.get_barrier_semaphore()
    partners = [here.sibling]
    partners += [here.along(axis, step) for axis in "xyz" for step in (1, 2, 3)]
    for device in partners:
        pl.semaphore_signal(barrier, inc=1, device_id=device, device_id_type=MESH)

    consts[0] = 0.5 * jnp.exp(jnp.full((8, width), log_scale[0], F32))
    consts[1] = jnp.full((8, width), 0.5 * bias[0], F32)
    h, shift = consts[0, 0:1, :], consts[1, 0:1, :]
    inputs = (fine_rows, coarse_rows)

    def embed(which, far, part, head_ref):
        at = pl.ds(part * half, half)
        proj = dot(rows_keep[which, pl.ds(far * rows + part * half, half)], head_ref[...], NN)
        inv = lax.rsqrt(jnp.sum(proj * proj, axis=-1, keepdims=True) + EPS)
        unit = proj * inv
        unit_keep[which, far, at] = unit
        inv_keep[which, far, at] = inv
        return unit.astype(BF16)

    for which in (0, 1):
        rows_keep[which, pl.ds(0, rows)] = inputs[which][...]
    pl.semaphore_wait(barrier, len(partners))
    far_device = (here.other_hi, here.other_lo)
    for part in (0, 1):
        for which in (0, 1):
            copies.start(
                f"z{which}{part}",
                (rows_keep, which, pl.ds(part * half, half)),
                (rows_keep, which, pl.ds(rows + part * half, half)),
                far_device[which],
            )

    def send_both(tag, axis, buf, at, order_plus, order_minus):
        for p in order_plus:
            copies.start(f"{tag}+{p}", (buf, at, slot_half(0, p)), (buf, at, slot_half(-1, p)), here.along(axis, 1))
        for p in order_minus:
            copies.start(f"{tag}-{p}", (buf, at, slot_half(0, p)), (buf, at, slot_half(1, p)), here.along(axis, 3))

    def pass_plus(tag, axis, buf, at):
        copies.wait(tag + "+0")
        copies.start(tag + "++", (buf, at, slot_half(-1, 0)), (buf, at, slot_half(2, 0)), here.along(axis, 1))

    def pass_minus(tag, axis, buf, at):
        copies.wait(tag + "-1")
        copies.start(tag + "--", (buf, at, slot_half(1, 1)), (buf, at, slot_half(2, 1)), here.along(axis, 3))

    def sib_near(tag, at):
        copies.wait(tag + "+1")
        copies.start(tag + "+s", (fine_all, at, slot(-1)), (fine_all, at + 1, slot(-1)), here.sibling)
        copies.wait(tag + "-0")
        copies.start(tag + "-s", (fine_all, at, slot(1)), (fine_all, at + 1, slot(1)), here.sibling)

    def sib_far(tag, at):
        copies.wait(tag + "++", tag + "--")
        copies.start(tag + "2s", (fine_all, at, slot(2)), (fine_all, at + 1, slot(2)), here.sibling)

    for p in (0, 1):
        fine_all[0, slot_half(0, p)] = embed(0, 0, p, fine_head)
    send_both("fx", "x", fine_all, 0, (0, 1), (1, 0))
    copies.start("fs", (fine_all, 0, slot(0)), (fine_all, 1, slot(0)), here.sibling)
    for p in (0, 1):
        coarse_all[0, slot_half(0, p)] = embed(1, 0, p, coarse_head)
    send_both("cy", "y", coarse_all, 0, (0, 1), (1, 0))

    coarse_acc[...] = jnp.zeros_like(coarse_acc)
    loss_acc[...] = jnp.zeros_like(loss_acc)

    fine_emb = fine_all[0, slot(0)].astype(F32)
    coarse_emb = coarse_all[0, slot(0)].astype(F32)
    arg = jnp.sum(fine_emb * coarse_emb, axis=-1, keepdims=True) * consts[0, 0:1, 0:1] + consts[1, 0:1, 0:1]
    tanh = jnp.tanh(arg)
    delta = (tanh - 1.0).astype(BF16).astype(F32) - (1.0 + tanh).astype(BF16).astype(F32)
    own_sum[0] = delta * coarse_emb
    own_sum[1] = delta * fine_emb
    diagonal = jnp.sum(2.0 * arg, axis=0, keepdims=True)

    pass_plus("fx", "x", fine_all, 0)
    pass_plus("cy", "y", coarse_all, 0)
    pass_minus("fx", "x", fine_all, 0)
    pass_minus("cy", "y", coarse_all, 0)
    for p in (0, 1):
        copies.wait(f"z0{p}")
        fine_all[2, slot_half(0, p)] = embed(0, 1, p, fine_head)
        for sign, step in (("+", 1), ("-", 3)):
            copies.start(f"gx{sign}{p}", (fine_all, 2, slot_half(0, p)), (fine_all, 2, slot_half(-step, p)), here.along("x", step))
        copies.wait(f"z1{p}")
        coarse_all[1, slot_half(0, p)] = embed(1, 1, p, coarse_head)
        for sign, step in (("+", 1), ("-", 3)):
            copies.start(f"dy{sign}{p}", (coarse_all, 1, slot_half(0, p)), (coarse_all, 1, slot_half(-step, p)), here.along("y", step))
    sib_near("fx", 0)
    copies.start("gs", (fine_all, 2, slot(0)), (fine_all, 3, slot(0)), here.sibling)
    for which in (0, 1):
        copies.start(f"rows{which}", (rows_keep, which, pl.ds(0, 2 * rows)), (rows_keep, which, pl.ds(2 * rows, 2 * rows)), here.sibling)
    fine_acc[...] = jnp.zeros_like(fine_acc)
    copies.wait("cy+1", "cy-0", "cy++", "cy--")
    sib_far("fx", 0)

    def tile(fg, cg):
        cols = coarse_all[cg]
        n = 256
        coefs = []
        for j in range(4 * rows // n):
            at = pl.ds(j * n, n)
            t = jnp.tanh(dot(fine_all[fg, at], cols, NT) * h + shift)
            coef = (1.0 + t).astype(BF16)
            rest = 1.0 - t
            eighth = n // 8
            p = [rest[i * eighth : (i + 1) * eighth] for i in range(8)]
            p = ((p[0] * p[1]) * (p[2] * p[3])) * ((p[4] * p[5]) * (p[6] * p[7]))
            p = jnp.log(p * (1.0 / 256.0))
            loss_acc[...] -= (p[0:8] + p[8:16]) + (p[16:24] + p[24:32])
            fine_acc[fg, at] += dot(coef, cols, NN)
            coefs.append(coef)
        coarse_acc[cg] += dot(jnp.concatenate(coefs, 0), fine_all[fg], TN)

    def to_sibling(k):
        sib_out[k] = fine_acc[2 * k + 1].astype(BF16)
        copies.start(f"sum_s{k}", (sib_out, k), (sib_in, k), here.sibling)

    def ring_start(tag, axis, r, acc, a, other):
        def total(step, p):
            value = acc[a, slot_half(step, p)]
            return value if other is None else value + sib_in[other, slot_half(step, p)].astype(F32)

        plus, minus = here.along(axis, 1), here.along(axis, 3)
        half_out[r, upper] = total(2, 0).astype(BF16)
        copies.start(tag + "h+", (half_out, r, upper), (half_in, r, upper), plus)
        half_out[r, lower] = total(2, 1).astype(BF16)
        copies.start(tag + "h-", (half_out, r, lower), (half_in, r, lower), minus)
        full_out[r, 0, lower] = total(1, 1).astype(BF16)
        copies.start(tag + "f+1", (full_out, r, 0, lower), (full_in, r, 0, lower), plus)
        full_out[r, 1, upper] = total(3, 0).astype(BF16)
        copies.start(tag + "f-0", (full_out, r, 1, upper), (full_in, r, 1, upper), minus)
        if other is not None:
            for step, p in ((1, 0), (3, 1), (0, 0), (0, 1)):
                acc[a, slot_half(step, p)] = total(step, p)

    def ring_middle(tag, axis, r, acc, a):
        copies.wait(tag + "h+")
        full_out[r, 0, upper] = (acc[a, slot_half(1, 0)] + half_in[r, upper].astype(F32)).astype(BF16)
        copies.start(tag + "f+0", (full_out, r, 0, upper), (full_in, r, 0, upper), here.along(axis, 1))
        copies.wait(tag + "h-")
        full_out[r, 1, lower] = (acc[a, slot_half(3, 1)] + half_in[r, lower].astype(F32)).astype(BF16)
        copies.start(tag + "f-1", (full_out, r, 1, lower), (full_in, r, 1, lower), here.along(axis, 3))

    def ring_end(tag, r, acc, a):
        copies.wait(tag + "f+0", tag + "f+1", tag + "f-0", tag + "f-1")
        return acc[a, slot(0)] + full_in[r, 0].astype(F32) + full_in[r, 1].astype(F32)

    def hop(which, value):
        hop_out[which] = value.astype(BF16)
        copies.start(f"hop{which}", (hop_out, which), (hop_in, which), far_device[which])

    def step(t, carry):
        @pl.when(t == 1)
        def _():
            pass_plus("gx", "x", fine_all, 2)
            pass_plus("dy", "y", coarse_all, 1)
            copies.wait("fs", "fx+s", "fx-s", "fx2s")

        @pl.when(t == 2)
        def _():
            pass_minus("gx", "x", fine_all, 2)
            pass_minus("dy", "y", coarse_all, 1)
            sib_near("gx", 2)
            sib_far("gx", 2)

        @pl.when(t == 3)
        def _():
            copies.wait("gs", "gx+s", "gx-s", "gx2s")

        @pl.when(t == 4)
        def _():
            ring_start("c0", "y", 2, coarse_acc, 0, None)
            copies.wait("dy+1", "dy-0", "dy++", "dy--")

        @pl.when(t == 5)
        def _():
            to_sibling(1)
            ring_middle("c0", "y", 2, coarse_acc, 0)

        @pl.when(t == 6)
        def _():
            copies.wait("sum_s1")
            ring_start("f1", "x", 1, fine_acc, 2, 1)
            own_sum[1] += ring_end("c0", 2, coarse_acc, 0)

        @pl.when(t == 7)
        def _():
            to_sibling(0)
            ring_middle("f1", "x", 1, fine_acc, 2)

        late = t // 4
        tile(t + late * (7 - 2 * t), late)
        return carry

    lax.fori_loop(0, 8, step, 0)

    def back(which, far, value):
        unit, inv = unit_keep[which, far], inv_keep[which, far]
        grad = value * h
        inner = jnp.sum(unit * grad, axis=-1, keepdims=True)
        return (inv * (grad - unit * inner)).astype(BF16)

    def keep(which, far, value):
        dp = back(which, far, value)
        for i in (0, 1):
            dp_keep[which, i, pl.ds(far * rows, rows)] = dp[:, i * wide : (i + 1) * wide]

    def dp_to_sibling(which):
        other = 1 - here.core
        copies.start(f"dp{which}", (dp_keep, which, other, pl.ds(0, 2 * rows)), (dp_keep, which, other, pl.ds(2 * rows, 2 * rows)), here.sibling)

    def grad_to_out(which, value, head_ref, out):
        grad_keep[which] = dot(back(which, 0, value), head_ref[...], NT)
        return pltpu.make_async_copy(grad_keep.at[which], out, local_sem.at[which])

    copies.wait("sum_s0")
    ring_start("f0", "x", 0, fine_acc, 0, 0)
    ring_start("c1", "y", 3, coarse_acc, 1, None)
    value = ring_end("f1", 1, fine_acc, 2)
    hop(0, value)
    keep(0, 1, value)

    loss = loss_acc[:, 0:128]
    for i in range(1, width // 128):
        loss = loss + loss_acc[:, i * 128 : (i + 1) * 128]
    at_origin = (lax.broadcasted_iota(jnp.int32, (8, 128), 0) + lax.broadcasted_iota(jnp.int32, (8, 128), 1)) == 0
    loss = loss - jnp.where(at_origin, diagonal, 0.0)
    loss_parts[0, 0] = loss
    copies.start("loss_s", (loss_parts, 0, 0), (loss_parts, 0, 1), here.sibling)

    def loss_round(r, axis, place):
        if r == 1:
            copies.wait("loss_s")
            value = loss_parts[0, 0] + loss_parts[0, 1]
        else:
            copies.wait(*[f"loss{r - 1}{d}" for d in (1, 2, 3)])
            q = loss_parts
            value = (q[r - 1, 0] + q[r - 1, 1]) + (q[r - 1, 2] + q[r - 1, 3])
        if axis is None:
            return value
        loss_parts[r, place] = value
        for d in (1, 2, 3):
            copies.start(f"loss{r}{d}", (loss_parts, r, place), (loss_parts, r, place), here.along(axis, d))

    ring_middle("f0", "x", 0, fine_acc, 0)
    ring_middle("c1", "y", 3, coarse_acc, 1)
    loss_round(1, "x", here.x)
    keep(1, 0, own_sum[1])
    value = ring_end("f0", 0, fine_acc, 0) + own_sum[0]
    own_sum[0] = value
    keep(0, 0, value)
    dp_to_sibling(0)
    value = ring_end("c1", 3, coarse_acc, 1)
    keep(1, 1, value)
    dp_to_sibling(1)
    hop(1, value)
    loss_round(2, "y", here.y)

    place = {"x": here.x, "y": here.y, "z": here.z}
    core = here.core
    n = rows // 4
    for which in (0, 1):
        copies.wait(f"rows{which}", f"dp{which}")
        value = dot(rows_keep[which], dp_keep[which, core], TN)
        for q in range(3):
            for j in range(4):
                part_out[q, j, which] = value[j * rows : (j + 1) * rows, q * 128 : (q + 1) * 128].astype(BF16)
    for d in (1, 3, 2):
        for q, (first, _, _) in enumerate(ORDERS):
            copies.start(f"part{q}{d}", (part_out, q, (place[first] + d) % 4), (part_in, q, d - 1), here.along(first, d))

    copies.wait("hop0")
    fine_copy = grad_to_out(0, own_sum[0] + hop_in[0].astype(F32), fine_head, fine_grad_out)
    fine_copy.start()
    copies.wait("hop1")
    coarse_copy = grad_to_out(1, own_sum[1] + hop_in[1].astype(F32), coarse_head, coarse_grad_out)
    coarse_copy.start()

    for q, (first, second, _) in enumerate(ORDERS):
        copies.wait(*[f"part{q}{d}" for d in (1, 2, 3)])
        value = part_out[q, place[first]].astype(F32)
        for d in range(3):
            value = value + part_in[q, d].astype(F32)
        for j in range(4):
            quarter_out[q, j] = value[:, j * n : (j + 1) * n].astype(BF16)
        for d in (1, 3, 2):
            copies.start(f"quarter{q}{d}", (quarter_out, q, (place[second] + d) % 4), (quarter_in, q, d - 1), here.along(second, d))
    loss_round(3, "z", here.z)
    for q, (_, second, third) in enumerate(ORDERS):
        copies.wait(*[f"quarter{q}{d}" for d in (1, 2, 3)])
        value = quarter_out[q, place[second]].astype(F32)
        for d in range(3):
            value = value + quarter_in[q, d].astype(F32)
        column[q, place[third]] = value.astype(BF16)
        mine = (column, q, place[third])
        for d in (1, 3, 2):
            copies.start(f"column{q}{d}", mine, mine, here.along(third, d))
    for q, (first, second, third) in enumerate(ORDERS):
        copies.wait(*[f"column{q}{d}" for d in (1, 2, 3)])
        value = column[q, 0].astype(F32)
        for i in range(1, 4):
            value = value + column[q, i].astype(F32)
        heads[core, q, place[first], place[second]] = value.astype(BF16)
        mine = (heads, core, q, place[first], place[second])
        for d in (1, 3, 2):
            copies.start(f"back{q}{d}", mine, mine, here.along(second, d))
    loss_out[...] = loss_round(4, None, None)
    for q, (first, second, _) in enumerate(ORDERS):
        copies.wait(*[f"back{q}{d}" for d in (1, 2, 3)])
        mine = (heads, core, q, place[first])
        for d in (1, 3, 2):
            copies.start(f"spread{q}{d}", mine, mine, here.along(first, d))
    for q in range(3):
        copies.wait(*[f"spread{q}{d}" for d in (1, 2, 3)])
        copies.start(f"share{q}", (heads, core, q), (heads, core, q), here.sibling)
    mine_copy = pltpu.make_async_copy(heads.at[core], heads_out.at[core], local_sem.at[2])
    mine_copy.start()
    copies.wait("share0", "share1", "share2")
    other_copy = pltpu.make_async_copy(heads.at[1 - core], heads_out.at[1 - core], local_sem.at[3])
    other_copy.start()
    copies.finish()
    fine_copy.wait()
    coarse_copy.wait()
    mine_copy.wait()
    other_copy.wait()


def place_results(pairs, loss_in, fine_in, coarse_in, heads, loss, fine_grad, coarse_grad, fine_head_grad, coarse_head_grad):
    loss[0] = jnp.sum(loss_in[...]) * (1.0 / pairs)
    fine_grad[...] = fine_in[...]
    coarse_grad[...] = coarse_in[...]
    halves, parts, _, pieces, _, n, lanes = heads.shape
    for side in range(halves):
        for q in range(parts):
            cols = pl.ds((side * parts + q) * lanes, lanes)
            for j in range(pieces):
                at = pl.ds(j * n, n)
                fine_head_grad[at, cols] = heads[side, q, 0, j, 0].astype(F32)
                coarse_head_grad[at, cols] = heads[side, q, 0, j, 1].astype(F32)


def shards(fine_rows, coarse_rows, fine_head, coarse_head, log_scale, bias):
    rows, width = fine_rows.shape
    wide, n = width // 2, rows // 4
    vmem = pl.BlockSpec(memory_space=pltpu.VMEM)
    smem = pl.BlockSpec(memory_space=pltpu.SMEM)
    anywhere = pl.BlockSpec(memory_space=pl.ANY)
    scratch = [
        VMEM((4, 4 * rows, width), BF16),
        VMEM((2, 4 * rows, width), BF16),
        VMEM((4, 4 * rows, width), F32),
        VMEM((2, 4 * rows, width), F32),
        VMEM((2, 2, rows, width), F32),
        VMEM((2, 2, rows, 1), F32),
        VMEM((2, 4 * rows, width), BF16),
        VMEM((2, 8, width), F32),
        VMEM((8, width), F32),
        VMEM((2, 4 * rows, width), BF16),
        VMEM((2, 4 * rows, width), BF16),
        VMEM((4, rows, width), BF16),
        VMEM((4, rows, width), BF16),
        VMEM((4, 2, rows, width), BF16),
        VMEM((4, 2, rows, width), BF16),
        VMEM((2, rows, width), BF16),
        VMEM((2, rows, width), BF16),
        VMEM((2, rows, width), F32),
        VMEM((2, 2, 4 * rows, wide), BF16),
        VMEM((2, rows, width), F32),
        VMEM((3, 4, 2, rows, 128), BF16),
        VMEM((3, 3, 2, rows, 128), BF16),
        VMEM((3, 4, 2, n, 128), BF16),
        VMEM((3, 3, 2, n, 128), BF16),
        VMEM((3, 4, 2, n, 128), BF16),
        VMEM((2, 3, 4, 4, 2, n, 128), BF16),
        VMEM((4, 4, 8, 128), F32),
        pltpu.SemaphoreType.DMA((N_COPIES,)),
        pltpu.SemaphoreType.DMA((N_COPIES,)),
        pltpu.SemaphoreType.DMA((4,)),
    ]
    tokens = rows * lax.axis_size("grp") * lax.axis_size("mem")
    pair_flops = 6 * (16 * rows) * (8 * rows) * width
    grad = jax.ShapeDtypeStruct((rows, width), F32)
    head = jax.ShapeDtypeStruct((width, width), F32)
    loss, fine_grad, coarse_grad, heads = pl.pallas_call(
        kernel,
        out_shape=(
            jax.ShapeDtypeStruct((8, 128), F32),
            grad,
            grad,
            jax.ShapeDtypeStruct((2, 3, 4, 4, 2, n, 128), BF16),
        ),
        in_specs=[vmem, vmem, vmem, vmem, smem, smem],
        out_specs=(vmem, anywhere, anywhere, anywhere),
        scratch_shapes=scratch,
        cost_estimate=pl.CostEstimate(flops=pair_flops, bytes_accessed=tokens * width, transcendentals=0),
        compiler_params=pltpu.CompilerParams(collective_id=0, has_side_effects=True, vmem_limit_bytes=60 * 2**20),
    )(fine_rows, coarse_rows, fine_head, coarse_head, log_scale, bias)

    def place(*refs):
        place_results(float(tokens) ** 2, *refs)

    by_rows = pl.BlockSpec((rows, width), lambda i: (i, 0))
    by_quarters = pl.BlockSpec((n, width), lambda i: (i, 0))
    return pl.pallas_call(
        place,
        grid=(4,),
        out_shape=(jax.ShapeDtypeStruct((1,), F32), grad, grad, head, head),
        in_specs=[
            pl.BlockSpec((8, 128), lambda i: (0, 0)),
            by_quarters,
            by_quarters,
            pl.BlockSpec((2, 3, 1, 4, 2, n, 128), lambda i: (0, 0, i, 0, 0, 0, 0)),
        ],
        out_specs=(smem, by_quarters, by_quarters, by_rows, by_rows),
    )(loss, fine_grad, coarse_grad, heads)


def solution(mesh):
    placed = (P(("grp", "mem"), None), P(("grp", "mem"), None), P(), P(), P(), P())
    return jax.shard_map(
        shards,
        mesh=mesh,
        in_specs=placed,
        out_specs=(P(), P(("grp", "mem"), None), P(("grp", "mem"), None), P(), P()),
        check_vma=False,
    )
```

```python
import jax
import jax.numpy as jnp
from jax import lax
from jax.experimental import pallas as pl
from jax.experimental.pallas import tpu as pltpu
from jax.sharding import PartitionSpec as P

MESH = pl.DeviceIdType.MESH
EPS = 1e-06
F32 = jnp.float32
BF16 = jnp.bfloat16
VMEM = pltpu.VMEM


def dot(a, b, dims):
    return lax.dot_general(a, b, (dims, ((), ())), preferred_element_type=F32)


NN = ((1,), (0,))
NT = ((1,), (1,))
TN = ((0,), (0,))


class Place:
    def __init__(self):
        grp, mem = lax.axis_index("grp"), lax.axis_index("mem")
        self.core = mem % 2
        self.x, self.y = (mem // 2) % 4, grp % 4
        self.z = (mem // 8) * 2 + grp // 4
        self.steps = {("x", d): self.at(dx=d) for d in (1, 2, 3)}
        self.steps |= {("y", d): self.at(dy=d) for d in (1, 2, 3)}
        self.steps |= {("z", d): self.at(z=(self.z + d) % 4) for d in (1, 2, 3)}
        self.sibling = self.at(core=1 - self.core)
        self.other_hi = self.steps["z", 2]
        self.other_lo = self.at(z=self.z + 1 - 2 * (self.z % 2))

    def at(self, dx=0, dy=0, z=None, core=None):
        x, y = (self.x + dx) % 4, (self.y + dy) % 4
        z = self.z if z is None else z
        core = self.core if core is None else core
        return ((z % 2) * 4 + y, (z // 2) * 8 + x * 2 + core)

    def along(self, axis, step):
        return self.steps[axis, step]


def view(ref, *index):
    return ref.at[index] if index else ref


class Copies:
    def __init__(self, send_sem, recv_sem):
        self.send_sem, self.recv_sem = send_sem, recv_sem
        self.made, self.sent = {}, set()

    def start(self, name, src, dst, device):
        index = len(self.made)
        assert name not in self.made and index < N_COPIES

        def make():
            return pltpu.make_async_remote_copy(
                src_ref=view(*src),
                dst_ref=view(*dst),
                send_sem=self.send_sem.at[index],
                recv_sem=self.recv_sem.at[index],
                device_id=device,
                device_id_type=MESH,
            )

        self.made[name] = make
        make().start()

    def wait(self, *names):
        for name in names:
            self.made[name]().wait_recv()

    def leave(self, *names):
        for name in names:
            self.sent.add(name)
            self.made[name]().wait_send()

    def finish(self):
        self.leave(*[name for name in self.made if name not in self.sent])


N_COPIES = 144
ORDERS = (("x", "y", "z"), ("y", "z", "x"), ("z", "x", "y"))


def kernel(
    fine_rows,
    coarse_rows,
    fine_head,
    coarse_head,
    log_scale,
    bias,
    loss_out,
    fine_grad_out,
    coarse_grad_out,
    heads_out,
    fine_all,
    coarse_all,
    fine_acc,
    coarse_acc,
    unit_keep,
    inv_keep,
    rows_keep,
    consts,
    loss_acc,
    sib_out,
    sib_in,
    half_out,
    half_in,
    full_out,
    full_in,
    hop_out,
    hop_in,
    own_sum,
    dp_keep,
    share_out,
    share_in,
    part_out,
    part_in,
    quarter_out,
    quarter_in,
    column,
    heads,
    loss_parts,
    send_sem,
    recv_sem,
    local_sem,
):
    rows, width = fine_rows.shape
    half = rows // 2
    wide = width // 2
    here = Place()
    copies = Copies(send_sem, recv_sem)
    upper, lower = pl.ds(0, half), pl.ds(half, half)

    def slot(step):
        return pl.ds((step % 4) * rows, rows)

    def slot_half(step, which):
        return pl.ds((step % 4) * rows + which * half, half)

    barrier = pltpu.get_barrier_semaphore()
    partners = [here.sibling]
    partners += [here.along(axis, step) for axis in "xyz" for step in (1, 2, 3)]
    for device in partners:
        pl.semaphore_signal(barrier, inc=1, device_id=device, device_id_type=MESH)

    consts[0] = 0.5 * jnp.exp(jnp.full((8, width), log_scale[0], F32))
    consts[1] = jnp.full((8, width), 0.5 * bias[0], F32)
    h, shift = consts[0, 0:1, :], consts[1, 0:1, :]
    inputs = (fine_rows, coarse_rows)

    far_rows = 4 * rows

    def embed(which, start, keep_unit=False):
        at = pl.ds(start, rows)
        proj = dot(rows_keep[which, at], (fine_head, coarse_head)[which][...], NN)
        inv = lax.rsqrt(jnp.sum(proj * proj, axis=-1, keepdims=True) + EPS)
        unit = proj * inv
        if keep_unit:
            unit_keep[which] = unit
        inv_keep[which, at] = inv
        return unit.astype(BF16)

    rows_keep[0, slot(0)] = fine_rows[...]
    rows_keep[1, pl.ds(far_rows, rows)] = coarse_rows[...]
    pl.semaphore_wait(barrier, len(partners))
    far_device = (here.other_hi, here.other_lo)

    def to_far(which, start, end):
        for p in (0, 1):
            copies.start(
                f"z{which}{p}",
                (rows_keep, which, pl.ds(start + p * half, half)),
                (rows_keep, which, pl.ds(end + p * half, half)),
                far_device[which],
            )

    def send_both(tag, axis, buf, at, order_plus, order_minus):
        for p in order_plus:
            copies.start(f"{tag}+{p}", (buf, at, slot_half(0, p)), (buf, at, slot_half(-1, p)), here.along(axis, 1))
        for p in order_minus:
            copies.start(f"{tag}-{p}", (buf, at, slot_half(0, p)), (buf, at, slot_half(1, p)), here.along(axis, 3))

    def pass_plus(tag, axis, buf, at):
        copies.wait(tag + "+0")
        copies.start(tag + "++", (buf, at, slot_half(-1, 0)), (buf, at, slot_half(2, 0)), here.along(axis, 1))

    def pass_minus(tag, axis, buf, at):
        copies.wait(tag + "-1")
        copies.start(tag + "--", (buf, at, slot_half(1, 1)), (buf, at, slot_half(2, 1)), here.along(axis, 3))

    def sib_near(tag, at):
        copies.wait(tag + "+1")
        copies.start(tag + "+s", (fine_all, at, slot(-1)), (fine_all, at + 1, slot(-1)), here.sibling)
        copies.wait(tag + "-0")
        copies.start(tag + "-s", (fine_all, at, slot(1)), (fine_all, at + 1, slot(1)), here.sibling)

    def sib_far(tag, at):
        copies.wait(tag + "++", tag + "--")
        copies.start(tag + "2s", (fine_all, at, slot(2)), (fine_all, at + 1, slot(2)), here.sibling)

    to_far(0, 0, far_rows)
    send_both("fx", "x", rows_keep, 0, (0, 1), (1, 0))
    to_far(1, far_rows, 0)
    coarse_all[0, slot(0)] = embed(1, far_rows, True)
    send_both("cy", "y", coarse_all, 0, (0, 1), (1, 0))
    fine_all[0, slot(0)] = embed(0, 0, True)
    copies.start("fs", (fine_all, 0, slot(0)), (fine_all, 1, slot(0)), here.sibling)

    coarse_acc[...] = jnp.zeros_like(coarse_acc)
    fine_acc[...] = jnp.zeros_like(fine_acc)
    loss_acc[...] = jnp.zeros_like(loss_acc)

    fine_emb = fine_all[0, slot(0)].astype(F32)
    coarse_emb = coarse_all[0, slot(0)].astype(F32)
    arg = jnp.sum(fine_emb * coarse_emb, axis=-1, keepdims=True) * consts[0, 0:1, 0:1] + consts[1, 0:1, 0:1]
    tanh = jnp.tanh(arg)
    delta = (tanh - 1.0).astype(BF16).astype(F32) - (1.0 + tanh).astype(BF16).astype(F32)
    own_sum[0] = delta * coarse_emb
    own_sum[1] = delta * fine_emb
    diagonal = jnp.sum(2.0 * arg, axis=0, keepdims=True)

    pass_plus("fx", "x", rows_keep, 0)
    pass_minus("fx", "x", rows_keep, 0)
    pass_plus("cy", "y", coarse_all, 0)
    pass_minus("cy", "y", coarse_all, 0)

    def near_fine(step, name):
        fine_all[0, slot(step)] = embed(0, (step % 4) * rows)
        copies.start(name, (fine_all, 0, slot(step)), (fine_all, 1, slot(step)), here.sibling)

    copies.wait("fx+1")
    near_fine(-1, "fx+s")
    copies.wait("fx-0")
    near_fine(1, "fx-s")
    copies.wait("z00", "z01")
    fine_all[2, slot(0)] = embed(0, far_rows)
    send_both("gx", "x", fine_all, 2, (0, 1), (1, 0))
    copies.start("gs", (fine_all, 2, slot(0)), (fine_all, 3, slot(0)), here.sibling)
    copies.wait("fx++", "fx--")
    near_fine(2, "fx2s")
    copies.wait("cy+1", "cy-0", "cy++", "cy--")

    def far_coarse(step):
        coarse_all[1, slot(step)] = embed(1, (step % 4) * rows)

    def tile(fg, cg):
        cols = coarse_all[cg]
        n = 256
        coefs = []
        for j in range(4 * rows // n):
            at = pl.ds(j * n, n)
            t = jnp.tanh(dot(fine_all[fg, at], cols, NT) * h + shift)
            coef = (1.0 + t).astype(BF16)
            rest = 1.0 - t
            eighth = n // 8
            p = [rest[i * eighth : (i + 1) * eighth] for i in range(8)]
            p = ((p[0] * p[1]) * (p[2] * p[3])) * ((p[4] * p[5]) * (p[6] * p[7]))
            p = jnp.log(p * (1.0 / 256.0))
            loss_acc[...] -= (p[0:8] + p[8:16]) + (p[16:24] + p[24:32])
            fine_acc[fg, at] += dot(coef, cols, NN)
            coefs.append(coef)
        coarse_acc[cg] += dot(jnp.concatenate(coefs, 0), fine_all[fg], TN)

    def to_sibling(k):
        if k == 0:
            copies.leave("sum_s1")
        sib_out[...] = fine_acc[2 * k + 1].astype(BF16)
        copies.start(f"sum_s{k}", (sib_out,), (sib_in, k), here.sibling)

    def ring_start(tag, axis, r, acc, a, other):
        def total(step, p):
            value = acc[a, slot_half(step, p)]
            return value if other is None else value + sib_in[other, slot_half(step, p)].astype(F32)

        if r % 2 == 0:
            earlier = {0: "f1", 2: "c0"}[r]
            copies.leave(*[earlier + name for name in ("h+", "h-", "f+0", "f+1", "f-0", "f-1")])
        plus, minus = here.along(axis, 1), here.along(axis, 3)
        half_out[r // 2, upper] = total(2, 0).astype(BF16)
        copies.start(tag + "h+", (half_out, r // 2, upper), (half_in, r, upper), plus)
        half_out[r // 2, lower] = total(2, 1).astype(BF16)
        copies.start(tag + "h-", (half_out, r // 2, lower), (half_in, r, lower), minus)
        full_out[r // 2, 0, lower] = total(1, 1).astype(BF16)
        copies.start(tag + "f+1", (full_out, r // 2, 0, lower), (full_in, r, 0, lower), plus)
        full_out[r // 2, 1, upper] = total(3, 0).astype(BF16)
        copies.start(tag + "f-0", (full_out, r // 2, 1, upper), (full_in, r, 1, upper), minus)

    def ring_own(acc, a, other):
        for step, p in ((1, 0), (3, 1), (0, 0), (0, 1)):
            at = slot_half(step, p)
            acc[a, at] += sib_in[other, at].astype(F32)

    def ring_middle(tag, axis, r, acc, a):
        copies.wait(tag + "h+")
        full_out[r // 2, 0, upper] = (acc[a, slot_half(1, 0)] + half_in[r, upper].astype(F32)).astype(BF16)
        copies.start(tag + "f+0", (full_out, r // 2, 0, upper), (full_in, r, 0, upper), here.along(axis, 1))
        copies.wait(tag + "h-")
        full_out[r // 2, 1, lower] = (acc[a, slot_half(3, 1)] + half_in[r, lower].astype(F32)).astype(BF16)
        copies.start(tag + "f-1", (full_out, r // 2, 1, lower), (full_in, r, 1, lower), here.along(axis, 3))

    def ring_end(tag, r, acc, a):
        copies.wait(tag + "f+0", tag + "f+1", tag + "f-0", tag + "f-1")
        return acc[a, slot(0)] + full_in[r, 0].astype(F32) + full_in[r, 1].astype(F32)

    def hop(which, value):
        hop_out[which] = value.astype(BF16)
        copies.start(f"hop{which}", (hop_out, which), (hop_in, which), far_device[which])

    def step(t, carry):
        @pl.when(t == 1)
        def _():
            copies.wait("z10", "z11")
            send_both("dy", "y", rows_keep, 1, (0, 1), (1, 0))
            pass_plus("gx", "x", fine_all, 2)
            pass_minus("gx", "x", fine_all, 2)
            copies.wait("fs", "fx+s", "fx-s", "fx2s")

        @pl.when(t == 2)
        def _():
            sib_near("gx", 2)
            pass_plus("dy", "y", rows_keep, 1)
            pass_minus("dy", "y", rows_keep, 1)
            far_coarse(0)
            sib_far("gx", 2)

        @pl.when(t == 3)
        def _():
            copies.wait("gs", "gx+s", "gx-s", "gx2s", "dy+1", "dy-0")
            far_coarse(-1)
            far_coarse(1)

        @pl.when(t == 4)
        def _():
            ring_start("c0", "y", 3, coarse_acc, 0, None)
            copies.wait("dy++", "dy--")
            far_coarse(2)

        @pl.when(t == 5)
        def _():
            to_sibling(1)
            ring_middle("c0", "y", 3, coarse_acc, 0)

        @pl.when(t == 6)
        def _():
            copies.wait("sum_s1")
            ring_start("f1", "x", 1, fine_acc, 2, 1)
            ring_own(fine_acc, 2, 1)
            own_sum[1] += ring_end("c0", 3, coarse_acc, 0)

        @pl.when(t == 7)
        def _():
            to_sibling(0)
            ring_middle("f1", "x", 1, fine_acc, 2)

        late = t // 4
        tile(t + late * (7 - 2 * t), late)
        return carry

    lax.fori_loop(0, 8, step, 0)

    def back(which, value, unit, inv):
        grad = value * h
        inner = jnp.sum(unit * grad, axis=-1, keepdims=True)
        return (inv * (grad - unit * inner)).astype(BF16)

    def keep(which, start, value, emb):
        at = pl.ds(start, rows)
        dp = back(which, value, emb.astype(F32), inv_keep[which, at])
        for i in (0, 1):
            dp_keep[which, i, at] = dp[:, i * wide : (i + 1) * wide]

    def grad_to_out(which, start, value, head_ref, out):
        dp = back(which, value, unit_keep[which], inv_keep[which, pl.ds(start, rows)])
        fine_acc[2 * which + 1, slot(0)] = dot(dp, head_ref[...], NT)
        return pltpu.make_async_copy(fine_acc.at[2 * which + 1, slot(0)], out, local_sem.at[which])

    core = here.core
    other = 1 - core

    ring_start("c1", "y", 2, coarse_acc, 1, None)
    copies.wait("sum_s0")
    fine_acc[0] += sib_in[0].astype(F32)
    ring_start("f0", "x", 0, fine_acc, 0, None)
    value = ring_end("f1", 1, fine_acc, 2)
    hop(0, value)
    keep(0, far_rows, value, fine_all[2, slot(0)])
    keep(1, far_rows, own_sum[1], coarse_all[0, slot(0)])
    for i in range(4):
        value = fine_acc[0, slot(i)]
        keep(0, i * rows, value + own_sum[0] if i == 0 else value, fine_all[0, slot(i)])
    share_out[0] = dot(rows_keep[0], dp_keep[0, other], TN).astype(BF16)
    for i in range(4):
        keep(1, i * rows, coarse_acc[1, slot(i)], coarse_all[1, slot(i)])
    copies.start("part_s0", (share_out, 0), (share_in, 0), here.sibling)
    share_out[1] = dot(rows_keep[1], dp_keep[1, other], TN).astype(BF16)
    copies.start("part_s1", (share_out, 1), (share_in, 1), here.sibling)
    ring_middle("c1", "y", 2, coarse_acc, 1)
    ring_middle("f0", "x", 0, fine_acc, 0)

    loss = loss_acc[:, 0:128]
    for i in range(1, width // 128):
        loss = loss + loss_acc[:, i * 128 : (i + 1) * 128]
    at_origin = (lax.broadcasted_iota(jnp.int32, (8, 128), 0) + lax.broadcasted_iota(jnp.int32, (8, 128), 1)) == 0
    loss = loss - jnp.where(at_origin, diagonal, 0.0)
    loss_parts[0, 0] = loss
    copies.start("loss_s", (loss_parts, 0, 0), (loss_parts, 0, 1), here.sibling)

    def loss_round(r, axis, place):
        if r == 1:
            copies.wait("loss_s")
            value = loss_parts[0, 0] + loss_parts[0, 1]
        else:
            copies.wait(*[f"loss{r - 1}{d}" for d in (1, 2, 3)])
            q = loss_parts
            value = (q[r - 1, 0] + q[r - 1, 1]) + (q[r - 1, 2] + q[r - 1, 3])
        if axis is None:
            return value
        loss_parts[r, place] = value
        for d in (1, 2, 3):
            copies.start(f"loss{r}{d}", (loss_parts, r, place), (loss_parts, r, place), here.along(axis, d))

    place = {"x": here.x, "y": here.y, "z": here.z}
    n = rows // 4
    for which in (0, 1):
        value = dot(rows_keep[which], dp_keep[which, core], TN)
        copies.wait(f"part_s{which}")
        value = value + share_in[which].astype(F32)
        for q in range(3):
            for j in range(4):
                part_out[q, j, which] = value[j * rows : (j + 1) * rows, q * 128 : (q + 1) * 128].astype(BF16)
    for d in (1, 3, 2):
        for q, (first, _, _) in enumerate(ORDERS):
            copies.start(f"part{q}{d}", (part_out, q, (place[first] + d) % 4), (part_in, q, d - 1), here.along(first, d))

    loss_round(1, "x", here.x)
    hop(1, ring_end("c1", 2, coarse_acc, 1))

    for q, (first, second, _) in enumerate(ORDERS):
        copies.wait(*[f"part{q}{d}" for d in (1, 2, 3)])
        value = part_out[q, place[first]].astype(F32)
        for d in range(3):
            value = value + part_in[q, d].astype(F32)
        for j in range(4):
            quarter_out[q, j] = value[:, j * n : (j + 1) * n].astype(BF16)
        for d in (1, 3, 2):
            copies.start(f"quarter{q}{d}", (quarter_out, q, (place[second] + d) % 4), (quarter_in, q, d - 1), here.along(second, d))
    loss_round(2, "y", here.y)
    own_sum[0] += ring_end("f0", 0, fine_acc, 0)
    for q, (_, second, third) in enumerate(ORDERS):
        copies.wait(*[f"quarter{q}{d}" for d in (1, 2, 3)])
        value = quarter_out[q, place[second]].astype(F32)
        for d in range(3):
            value = value + quarter_in[q, d].astype(F32)
        column[q, place[third]] = value.astype(BF16)
        mine = (column, q, place[third])
        for d in (1, 3, 2):
            copies.start(f"column{q}{d}", mine, mine, here.along(third, d))
    loss_round(3, "z", here.z)
    for q, (first, second, third) in enumerate(ORDERS):
        copies.wait(*[f"column{q}{d}" for d in (1, 2, 3)])
        value = column[q, 0].astype(F32)
        for i in range(1, 4):
            value = value + column[q, i].astype(F32)
        heads[core, q, place[first], place[second]] = value.astype(BF16)
        mine = (heads, core, q, place[first], place[second])
        for d in (1, 3, 2):
            copies.start(f"back{q}{d}", mine, mine, here.along(second, d))
    copies.wait("hop0")
    fine_copy = grad_to_out(0, 0, own_sum[0] + hop_in[0].astype(F32), fine_head, fine_grad_out)
    fine_copy.start()
    for q, (first, second, _) in enumerate(ORDERS):
        copies.wait(*[f"back{q}{d}" for d in (1, 2, 3)])
        mine = (heads, core, q, place[first])
        for d in (1, 3, 2):
            copies.start(f"spread{q}{d}", mine, mine, here.along(first, d))
    for q, (first, _, _) in enumerate(ORDERS):
        mine = (heads, core, q, place[first])
        copies.start(f"share{q}0", mine, mine, here.sibling)
    copies.wait("hop1")
    coarse_copy = grad_to_out(1, far_rows, own_sum[1] + hop_in[1].astype(F32), coarse_head, coarse_grad_out)
    coarse_copy.start()
    loss_out[...] = loss_round(4, None, None)
    for d in (1, 3, 2):
        for q, (first, _, _) in enumerate(ORDERS):
            copies.wait(f"spread{q}{d}")
            got = (heads, core, q, (place[first] + 4 - d) % 4)
            copies.start(f"share{q}{d}", got, got, here.sibling)
    mine_copy = pltpu.make_async_copy(heads.at[core], heads_out.at[core], local_sem.at[2])
    mine_copy.start()
    copies.wait(*[f"share{q}{d}" for q in range(3) for d in range(4)])
    other_copy = pltpu.make_async_copy(heads.at[1 - core], heads_out.at[1 - core], local_sem.at[3])
    other_copy.start()
    copies.finish()
    fine_copy.wait()
    coarse_copy.wait()
    mine_copy.wait()
    other_copy.wait()


def place_results(pairs, loss_in, fine_in, coarse_in, heads, loss, fine_grad, coarse_grad, fine_head_grad, coarse_head_grad):
    loss[0] = jnp.sum(loss_in[...]) * (1.0 / pairs)
    fine_grad[...] = fine_in[...]
    coarse_grad[...] = coarse_in[...]
    halves, parts, _, pieces, _, n, lanes = heads.shape
    for side in range(halves):
        for q in range(parts):
            cols = pl.ds((side * parts + q) * lanes, lanes)
            for j in range(pieces):
                at = pl.ds(j * n, n)
                fine_head_grad[at, cols] = heads[side, q, 0, j, 0].astype(F32)
                coarse_head_grad[at, cols] = heads[side, q, 0, j, 1].astype(F32)


def shards(fine_rows, coarse_rows, fine_head, coarse_head, log_scale, bias):
    rows, width = fine_rows.shape
    wide, n = width // 2, rows // 4
    vmem = pl.BlockSpec(memory_space=pltpu.VMEM)
    smem = pl.BlockSpec(memory_space=pltpu.SMEM)
    anywhere = pl.BlockSpec(memory_space=pl.ANY)
    scratch = [
        VMEM((4, 4 * rows, width), BF16),
        VMEM((2, 4 * rows, width), BF16),
        VMEM((4, 4 * rows, width), F32),
        VMEM((2, 4 * rows, width), F32),
        VMEM((2, rows, width), F32),
        VMEM((2, 5 * rows, 1), F32),
        VMEM((2, 5 * rows, width), BF16),
        VMEM((2, 8, width), F32),
        VMEM((8, width), F32),
        VMEM((4 * rows, width), BF16),
        VMEM((2, 4 * rows, width), BF16),
        VMEM((2, rows, width), BF16),
        VMEM((4, rows, width), BF16),
        VMEM((2, 2, rows, width), BF16),
        VMEM((4, 2, rows, width), BF16),
        VMEM((2, rows, width), BF16),
        VMEM((2, rows, width), BF16),
        VMEM((2, rows, width), F32),
        VMEM((2, 2, 5 * rows, wide), BF16),
        VMEM((2, width, wide), BF16),
        VMEM((2, width, wide), BF16),
        VMEM((3, 4, 2, rows, 128), BF16),
        VMEM((3, 3, 2, rows, 128), BF16),
        VMEM((3, 4, 2, n, 128), BF16),
        VMEM((3, 3, 2, n, 128), BF16),
        VMEM((3, 4, 2, n, 128), BF16),
        VMEM((2, 3, 4, 4, 2, n, 128), BF16),
        VMEM((4, 4, 8, 128), F32),
        pltpu.SemaphoreType.DMA((N_COPIES,)),
        pltpu.SemaphoreType.DMA((N_COPIES,)),
        pltpu.SemaphoreType.DMA((4,)),
    ]
    tokens = rows * lax.axis_size("grp") * lax.axis_size("mem")
    pair_flops = 6 * (16 * rows) * (8 * rows) * width
    grad = jax.ShapeDtypeStruct((rows, width), F32)
    head = jax.ShapeDtypeStruct((width, width), F32)
    loss, fine_grad, coarse_grad, heads = pl.pallas_call(
        kernel,
        out_shape=(
            jax.ShapeDtypeStruct((8, 128), F32),
            grad,
            grad,
            jax.ShapeDtypeStruct((2, 3, 4, 4, 2, n, 128), BF16),
        ),
        in_specs=[vmem, vmem, vmem, vmem, smem, smem],
        out_specs=(vmem, anywhere, anywhere, anywhere),
        scratch_shapes=scratch,
        cost_estimate=pl.CostEstimate(flops=pair_flops, bytes_accessed=tokens * width, transcendentals=0),
        compiler_params=pltpu.CompilerParams(collective_id=0, has_side_effects=True, vmem_limit_bytes=60 * 2**20),
    )(fine_rows, coarse_rows, fine_head, coarse_head, log_scale, bias)

    def place(*refs):
        place_results(float(tokens) ** 2, *refs)

    by_rows = pl.BlockSpec((rows, width), lambda i: (i, 0))
    by_quarters = pl.BlockSpec((n, width), lambda i: (i, 0))
    return pl.pallas_call(
        place,
        grid=(4,),
        out_shape=(jax.ShapeDtypeStruct((1,), F32), grad, grad, head, head),
        in_specs=[
            pl.BlockSpec((8, 128), lambda i: (0, 0)),
            by_quarters,
            by_quarters,
            pl.BlockSpec((2, 3, 1, 4, 2, n, 128), lambda i: (0, 0, i, 0, 0, 0, 0)),
        ],
        out_specs=(smem, by_quarters, by_quarters, by_rows, by_rows),
    )(loss, fine_grad, coarse_grad, heads)


def solution(mesh):
    placed = (P(("grp", "mem"), None), P(("grp", "mem"), None), P(), P(), P(), P())
    return jax.shard_map(
        shards,
        mesh=mesh,
        in_specs=placed,
        out_specs=(P(), P(("grp", "mem"), None), P(("grp", "mem"), None), P(), P()),
        check_vma=False,
    )
```

```python
import jax
import jax.numpy as jnp
from jax import lax
from jax.experimental import pallas as pl
from jax.experimental.pallas import tpu as pltpu
from jax.sharding import PartitionSpec as P

MESH = pl.DeviceIdType.MESH
EPS = 1e-06
F32 = jnp.float32
BF16 = jnp.bfloat16
VMEM = pltpu.VMEM


def dot(a, b, dims):
    return lax.dot_general(a, b, (dims, ((), ())), preferred_element_type=F32)


NN = ((1,), (0,))
NT = ((1,), (1,))
TN = ((0,), (0,))


class Place:
    def __init__(self):
        grp, mem = lax.axis_index("grp"), lax.axis_index("mem")
        self.core = mem % 2
        self.x, self.y = (mem // 2) % 4, grp % 4
        self.z = (mem // 8) * 2 + grp // 4
        self.steps = {("x", d): self.at(dx=d) for d in (1, 2, 3)}
        self.steps |= {("y", d): self.at(dy=d) for d in (1, 2, 3)}
        self.steps |= {("z", d): self.at(z=(self.z + d) % 4) for d in (1, 2, 3)}
        self.sibling = self.at(core=1 - self.core)
        self.other_hi = self.steps["z", 2]
        self.other_lo = self.at(z=self.z + 1 - 2 * (self.z % 2))

    def at(self, dx=0, dy=0, z=None, core=None):
        x, y = (self.x + dx) % 4, (self.y + dy) % 4
        z = self.z if z is None else z
        core = self.core if core is None else core
        return ((z % 2) * 4 + y, (z // 2) * 8 + x * 2 + core)

    def along(self, axis, step):
        return self.steps[axis, step]


def view(ref, *index):
    return ref.at[index] if index else ref


class Copies:
    def __init__(self, send_sem, recv_sem):
        self.send_sem, self.recv_sem = send_sem, recv_sem
        self.made, self.sent = {}, set()

    def start(self, name, src, dst, device):
        index = len(self.made)
        assert name not in self.made and index < N_COPIES

        def make():
            return pltpu.make_async_remote_copy(
                src_ref=view(*src),
                dst_ref=view(*dst),
                send_sem=self.send_sem.at[index],
                recv_sem=self.recv_sem.at[index],
                device_id=device,
                device_id_type=MESH,
            )

        self.made[name] = make
        make().start()

    def wait(self, *names):
        for name in names:
            self.made[name]().wait_recv()

    def leave(self, *names):
        for name in names:
            self.sent.add(name)
            self.made[name]().wait_send()

    def finish(self):
        self.leave(*[name for name in self.made if name not in self.sent])


N_COPIES = 144
ORDERS = (("x", "y", "z"), ("y", "z", "x"), ("z", "x", "y"))


def kernel(
    fine_rows,
    coarse_rows,
    fine_head,
    coarse_head,
    log_scale,
    bias,
    loss_out,
    fine_grad_out,
    coarse_grad_out,
    heads_out,
    fine_all,
    coarse_all,
    fine_acc,
    coarse_acc,
    unit_keep,
    inv_keep,
    rows_keep,
    consts,
    loss_acc,
    sib_out,
    sib_in,
    half_out,
    half_in,
    full_out,
    full_in,
    hop_out,
    hop_in,
    own_sum,
    dp_keep,
    share_out,
    share_in,
    part_out,
    part_in,
    quarter_out,
    quarter_in,
    column,
    heads,
    loss_parts,
    send_sem,
    recv_sem,
    local_sem,
):
    rows, width = fine_rows.shape
    half = rows // 2
    wide = width // 2
    here = Place()
    copies = Copies(send_sem, recv_sem)
    upper, lower = pl.ds(0, half), pl.ds(half, half)

    def slot(step):
        return pl.ds((step % 4) * rows, rows)

    def slot_half(step, which):
        return pl.ds((step % 4) * rows + which * half, half)

    barrier = pltpu.get_barrier_semaphore()
    partners = [here.sibling]
    partners += [here.along(axis, step) for axis in "xyz" for step in (1, 2, 3)]
    for device in partners:
        pl.semaphore_signal(barrier, inc=1, device_id=device, device_id_type=MESH)

    consts[0] = 0.5 * jnp.exp(jnp.full((8, width), log_scale[0], F32))
    consts[1] = jnp.full((8, width), 0.5 * bias[0], F32)
    h, shift = consts[0, 0:1, :], consts[1, 0:1, :]
    inputs = (fine_rows, coarse_rows)

    far_rows = 4 * rows

    def embed(which, start, keep_unit=False):
        at = pl.ds(start, rows)
        proj = dot(rows_keep[which, at], (fine_head, coarse_head)[which][...], NN)
        inv = lax.rsqrt(jnp.sum(proj * proj, axis=-1, keepdims=True) + EPS)
        unit = proj * inv
        if keep_unit:
            unit_keep[which] = unit
        inv_keep[which, at] = inv
        return unit.astype(BF16)

    rows_keep[0, slot(0)] = fine_rows[...]
    rows_keep[1, pl.ds(far_rows, rows)] = coarse_rows[...]
    pl.semaphore_wait(barrier, len(partners))
    far_device = (here.other_hi, here.other_lo)

    def to_far(which, start, end):
        for p in (0, 1):
            copies.start(
                f"z{which}{p}",
                (rows_keep, which, pl.ds(start + p * half, half)),
                (rows_keep, which, pl.ds(end + p * half, half)),
                far_device[which],
            )

    def send_both(tag, axis, buf, at, order_plus, order_minus):
        for p in order_plus:
            copies.start(f"{tag}+{p}", (buf, at, slot_half(0, p)), (buf, at, slot_half(-1, p)), here.along(axis, 1))
        for p in order_minus:
            copies.start(f"{tag}-{p}", (buf, at, slot_half(0, p)), (buf, at, slot_half(1, p)), here.along(axis, 3))

    def pass_plus(tag, axis, buf, at):
        copies.wait(tag + "+0")
        copies.start(tag + "++", (buf, at, slot_half(-1, 0)), (buf, at, slot_half(2, 0)), here.along(axis, 1))

    def pass_minus(tag, axis, buf, at):
        copies.wait(tag + "-1")
        copies.start(tag + "--", (buf, at, slot_half(1, 1)), (buf, at, slot_half(2, 1)), here.along(axis, 3))

    def sib_near(tag, at):
        copies.wait(tag + "+1")
        copies.start(tag + "+s", (fine_all, at, slot(-1)), (fine_all, at + 1, slot(-1)), here.sibling)
        copies.wait(tag + "-0")
        copies.start(tag + "-s", (fine_all, at, slot(1)), (fine_all, at + 1, slot(1)), here.sibling)

    def sib_far(tag, at):
        copies.wait(tag + "++", tag + "--")
        copies.start(tag + "2s", (fine_all, at, slot(2)), (fine_all, at + 1, slot(2)), here.sibling)

    to_far(0, 0, far_rows)
    send_both("fx", "x", rows_keep, 0, (0, 1), (1, 0))
    to_far(1, far_rows, 0)
    coarse_all[0, slot(0)] = embed(1, far_rows, True)
    send_both("cy", "y", coarse_all, 0, (0, 1), (1, 0))
    fine_all[0, slot(0)] = embed(0, 0, True)
    copies.start("fs", (fine_all, 0, slot(0)), (fine_all, 1, slot(0)), here.sibling)

    coarse_acc[...] = jnp.zeros_like(coarse_acc)
    fine_acc[...] = jnp.zeros_like(fine_acc)
    loss_acc[...] = jnp.zeros_like(loss_acc)

    fine_emb = fine_all[0, slot(0)].astype(F32)
    coarse_emb = coarse_all[0, slot(0)].astype(F32)
    arg = jnp.sum(fine_emb * coarse_emb, axis=-1, keepdims=True) * consts[0, 0:1, 0:1] + consts[1, 0:1, 0:1]
    tanh = jnp.tanh(arg)
    delta = (tanh - 1.0).astype(BF16).astype(F32) - (1.0 + tanh).astype(BF16).astype(F32)
    own_sum[0] = delta * coarse_emb
    own_sum[1] = delta * fine_emb
    diagonal = jnp.sum(2.0 * arg, axis=0, keepdims=True)

    pass_plus("fx", "x", rows_keep, 0)
    pass_minus("fx", "x", rows_keep, 0)
    pass_plus("cy", "y", coarse_all, 0)
    pass_minus("cy", "y", coarse_all, 0)

    def near_fine(step, name):
        fine_all[0, slot(step)] = embed(0, (step % 4) * rows)
        copies.start(name, (fine_all, 0, slot(step)), (fine_all, 1, slot(step)), here.sibling)

    copies.wait("z00", "z01")
    fine_all[2, slot(0)] = embed(0, far_rows)
    send_both("gx", "x", fine_all, 2, (0, 1), (1, 0))
    copies.wait("fx+1")
    near_fine(-1, "fx+s")
    copies.wait("fx-0")
    near_fine(1, "fx-s")
    copies.start("gs", (fine_all, 2, slot(0)), (fine_all, 3, slot(0)), here.sibling)
    copies.wait("fx++", "fx--")
    near_fine(2, "fx2s")
    copies.wait("cy+1", "cy-0", "cy++", "cy--")

    def far_coarse(step):
        coarse_all[1, slot(step)] = embed(1, (step % 4) * rows)

    def tile(fg, cg):
        cols = coarse_all[cg]
        n = 2 * rows
        coefs = []
        for j in range(4 * rows // n):
            at = pl.ds(j * n, n)
            t = jnp.tanh(dot(fine_all[fg, at], cols, NT) * h + shift)
            coef = (1.0 + t).astype(BF16)
            rest = 1.0 - t
            eighth = n // 8
            p = [rest[i * eighth : (i + 1) * eighth] for i in range(8)]
            p = ((p[0] * p[1]) * (p[2] * p[3])) * ((p[4] * p[5]) * (p[6] * p[7]))
            p = jnp.log(p * (1.0 / 256.0))
            for i in range(0, eighth, 8):
                loss_acc[...] -= p[i : i + 8]
            fine_acc[fg, at] += dot(coef, cols, NN)
            coefs.append(coef)
        coarse_acc[cg] += dot(jnp.concatenate(coefs, 0), fine_all[fg], TN)

    def to_sibling(k):
        if k == 0:
            copies.leave("sum_s1")
        sib_out[...] = fine_acc[2 * k + 1].astype(BF16)
        copies.start(f"sum_s{k}", (sib_out,), (sib_in, k), here.sibling)

    def ring_start(tag, axis, r, acc, a, other):
        def total(step, p):
            value = acc[a, slot_half(step, p)]
            return value if other is None else value + sib_in[other, slot_half(step, p)].astype(F32)

        if r % 2 == 0:
            earlier = {0: "f1", 2: "c0"}[r]
            copies.leave(*[earlier + name for name in ("h+", "h-", "f+0", "f+1", "f-0", "f-1")])
        plus, minus = here.along(axis, 1), here.along(axis, 3)
        half_out[r // 2, upper] = total(2, 0).astype(BF16)
        copies.start(tag + "h+", (half_out, r // 2, upper), (half_in, r, upper), plus)
        half_out[r // 2, lower] = total(2, 1).astype(BF16)
        copies.start(tag + "h-", (half_out, r // 2, lower), (half_in, r, lower), minus)
        full_out[r // 2, 0, lower] = total(1, 1).astype(BF16)
        copies.start(tag + "f+1", (full_out, r // 2, 0, lower), (full_in, r, 0, lower), plus)
        full_out[r // 2, 1, upper] = total(3, 0).astype(BF16)
        copies.start(tag + "f-0", (full_out, r // 2, 1, upper), (full_in, r, 1, upper), minus)

    def ring_own(acc, a, other):
        for step, p in ((1, 0), (3, 1), (0, 0), (0, 1)):
            at = slot_half(step, p)
            acc[a, at] += sib_in[other, at].astype(F32)

    def ring_middle(tag, axis, r, acc, a):
        copies.wait(tag + "h+")
        full_out[r // 2, 0, upper] = (acc[a, slot_half(1, 0)] + half_in[r, upper].astype(F32)).astype(BF16)
        copies.start(tag + "f+0", (full_out, r // 2, 0, upper), (full_in, r, 0, upper), here.along(axis, 1))
        copies.wait(tag + "h-")
        full_out[r // 2, 1, lower] = (acc[a, slot_half(3, 1)] + half_in[r, lower].astype(F32)).astype(BF16)
        copies.start(tag + "f-1", (full_out, r // 2, 1, lower), (full_in, r, 1, lower), here.along(axis, 3))

    def ring_end(tag, r, acc, a):
        copies.wait(tag + "f+0", tag + "f+1", tag + "f-0", tag + "f-1")
        return acc[a, slot(0)] + full_in[r, 0].astype(F32) + full_in[r, 1].astype(F32)

    def hop(which, value):
        hop_out[which] = value.astype(BF16)
        copies.start(f"hop{which}", (hop_out, which), (hop_in, which), far_device[which])

    def step(t, carry):
        @pl.when(t == 1)
        def _():
            pass_plus("gx", "x", fine_all, 2)
            pass_minus("gx", "x", fine_all, 2)
            copies.wait("z10", "z11")
            send_both("dy", "y", rows_keep, 1, (0, 1), (1, 0))
            copies.wait("fs", "fx+s", "fx-s", "fx2s")

        @pl.when(t == 2)
        def _():
            sib_near("gx", 2)
            far_coarse(0)
            sib_far("gx", 2)
            pass_plus("dy", "y", rows_keep, 1)
            pass_minus("dy", "y", rows_keep, 1)

        @pl.when(t == 3)
        def _():
            copies.wait("gs", "gx+s", "gx-s", "gx2s", "dy+1", "dy-0")
            far_coarse(-1)
            far_coarse(1)

        @pl.when(t == 4)
        def _():
            ring_start("c0", "y", 3, coarse_acc, 0, None)
            copies.wait("dy++", "dy--")
            far_coarse(2)

        @pl.when(t == 5)
        def _():
            to_sibling(1)

        @pl.when(t == 6)
        def _():
            copies.wait("sum_s1")
            ring_start("f1", "x", 1, fine_acc, 2, 1)
            ring_own(fine_acc, 2, 1)
            ring_middle("c0", "y", 3, coarse_acc, 0)

        @pl.when(t == 7)
        def _():
            to_sibling(0)
            ring_middle("f1", "x", 1, fine_acc, 2)

        late = t // 4
        tile(t + late * (7 - 2 * t), late)
        return carry

    lax.fori_loop(0, 8, step, 0)

    def back(value, unit, inv):
        inner = jnp.sum(unit * value, axis=-1, keepdims=True)
        return ((inv * h) * (value - unit * inner)).astype(BF16)

    def keep(which, start, value_at, buf, a, first):
        n = 32
        for i in range(0, rows, n):
            at = pl.ds(start + i, n)
            dp = back(value_at(i, n), buf[a, pl.ds(first + i, n)].astype(F32), inv_keep[which, at])
            for side in (0, 1):
                dp_keep[which, side, at] = dp[:, side * wide : (side + 1) * wide]

    def grad_to_out(which, start, value, head_ref, out):
        dp = back(value, unit_keep[which], inv_keep[which, pl.ds(start, rows)])
        fine_acc[2 * which + 1, slot(0)] = dot(dp, head_ref[...], NT)
        return pltpu.make_async_copy(fine_acc.at[2 * which + 1, slot(0)], out, local_sem.at[which])

    core = here.core
    other = 1 - core

    ring_start("c1", "y", 2, coarse_acc, 1, None)
    copies.wait("sum_s0")
    for i in range(4):
        fine_acc[0, slot(i)] += sib_in[0, slot(i)].astype(F32)
    ring_start("f0", "x", 0, fine_acc, 0, None)
    own_sum[1] += ring_end("c0", 3, coarse_acc, 0)
    keep(1, far_rows, lambda i, n: own_sum[1, pl.ds(i, n)], coarse_all, 0, 0)
    keep(1, 0, lambda i, n: coarse_acc[1, pl.ds(i, n)], coarse_all, 1, 0)
    keep(1, rows, lambda i, n: coarse_acc[1, pl.ds(rows + i, n)], coarse_all, 1, rows)
    keep(1, 2 * rows, lambda i, n: coarse_acc[1, pl.ds(2 * rows + i, n)], coarse_all, 1, 2 * rows)
    keep(1, 3 * rows, lambda i, n: coarse_acc[1, pl.ds(3 * rows + i, n)], coarse_all, 1, 3 * rows)
    share_out[1] = dot(rows_keep[1], dp_keep[1, other], TN).astype(BF16)
    keep(0, 0, lambda i, n: fine_acc[0, pl.ds(i, n)] + own_sum[0, pl.ds(i, n)], fine_all, 0, 0)
    keep(0, rows, lambda i, n: fine_acc[0, pl.ds(rows + i, n)], fine_all, 0, rows)
    keep(0, 2 * rows, lambda i, n: fine_acc[0, pl.ds(2 * rows + i, n)], fine_all, 0, 2 * rows)
    keep(0, 3 * rows, lambda i, n: fine_acc[0, pl.ds(3 * rows + i, n)], fine_all, 0, 3 * rows)
    copies.start("part_s1", (share_out, 1), (share_in, 1), here.sibling)
    ring_middle("c1", "y", 2, coarse_acc, 1)
    value = ring_end("f1", 1, fine_acc, 2)
    hop(0, value)
    fine_acc[2, slot(0)] = value
    keep(0, far_rows, lambda i, n: fine_acc[2, pl.ds(i, n)], fine_all, 2, 0)
    share_out[0] = dot(rows_keep[0], dp_keep[0, other], TN).astype(BF16)
    copies.start("part_s0", (share_out, 0), (share_in, 0), here.sibling)
    ring_middle("f0", "x", 0, fine_acc, 0)

    loss = loss_acc[:, 0:128]
    for i in range(1, width // 128):
        loss = loss + loss_acc[:, i * 128 : (i + 1) * 128]
    at_origin = (lax.broadcasted_iota(jnp.int32, (8, 128), 0) + lax.broadcasted_iota(jnp.int32, (8, 128), 1)) == 0
    loss = loss - jnp.where(at_origin, diagonal, 0.0)
    loss_parts[0, 0] = loss
    copies.start("loss_s", (loss_parts, 0, 0), (loss_parts, 0, 1), here.sibling)

    def loss_round(r, axis, place):
        if r == 1:
            copies.wait("loss_s")
            value = loss_parts[0, 0] + loss_parts[0, 1]
        else:
            copies.wait(*[f"loss{r - 1}{d}" for d in (1, 2, 3)])
            q = loss_parts
            value = (q[r - 1, 0] + q[r - 1, 1]) + (q[r - 1, 2] + q[r - 1, 3])
        if axis is None:
            return value
        loss_parts[r, place] = value
        for d in (1, 2, 3):
            copies.start(f"loss{r}{d}", (loss_parts, r, place), (loss_parts, r, place), here.along(axis, d))

    place = {"x": here.x, "y": here.y, "z": here.z}
    n = rows // 4
    for which in (1, 0):
        value = dot(rows_keep[which], dp_keep[which, core], TN)
        copies.wait(f"part_s{which}")
        value = value + share_in[which].astype(F32)
        for q in range(3):
            for j in range(4):
                part_out[q, j, which] = value[j * rows : (j + 1) * rows, q * 128 : (q + 1) * 128].astype(BF16)
    for d in (1, 3, 2):
        for q, (first, _, _) in enumerate(ORDERS):
            copies.start(f"part{q}{d}", (part_out, q, (place[first] + d) % 4), (part_in, q, d - 1), here.along(first, d))

    loss_round(1, "x", here.x)
    hop(1, ring_end("c1", 2, coarse_acc, 1))

    for q, (first, second, _) in enumerate(ORDERS):
        copies.wait(*[f"part{q}{d}" for d in (1, 2, 3)])
        value = part_out[q, place[first]].astype(F32)
        for d in range(3):
            value = value + part_in[q, d].astype(F32)
        for j in range(4):
            quarter_out[q, j] = value[:, j * n : (j + 1) * n].astype(BF16)
        for d in (1, 3, 2):
            copies.start(f"quarter{q}{d}", (quarter_out, q, (place[second] + d) % 4), (quarter_in, q, d - 1), here.along(second, d))
    loss_round(2, "y", here.y)
    own_sum[0] += ring_end("f0", 0, fine_acc, 0)
    for q, (_, second, third) in enumerate(ORDERS):
        copies.wait(*[f"quarter{q}{d}" for d in (1, 2, 3)])
        value = quarter_out[q, place[second]].astype(F32)
        for d in range(3):
            value = value + quarter_in[q, d].astype(F32)
        column[q, place[third]] = value.astype(BF16)
        mine = (column, q, place[third])
        for d in (1, 3, 2):
            copies.start(f"column{q}{d}", mine, mine, here.along(third, d))
    loss_round(3, "z", here.z)
    for q, (first, second, third) in enumerate(ORDERS):
        copies.wait(*[f"column{q}{d}" for d in (1, 2, 3)])
        value = column[q, 0].astype(F32)
        for i in range(1, 4):
            value = value + column[q, i].astype(F32)
        heads[core, q, place[first], place[second]] = value.astype(BF16)
        mine = (heads, core, q, place[first], place[second])
        for d in (1, 3, 2):
            copies.start(f"back{q}{d}", mine, mine, here.along(second, d))
    copies.wait("hop0")
    fine_copy = grad_to_out(0, 0, own_sum[0] + hop_in[0].astype(F32), fine_head, fine_grad_out)
    fine_copy.start()
    for q, (first, second, _) in enumerate(ORDERS):
        copies.wait(*[f"back{q}{d}" for d in (1, 2, 3)])
        mine = (heads, core, q, place[first])
        for d in (1, 3, 2):
            copies.start(f"spread{q}{d}", mine, mine, here.along(first, d))
    for q, (first, _, _) in enumerate(ORDERS):
        mine = (heads, core, q, place[first])
        copies.start(f"share{q}0", mine, mine, here.sibling)
    copies.wait("hop1")
    coarse_copy = grad_to_out(1, far_rows, own_sum[1] + hop_in[1].astype(F32), coarse_head, coarse_grad_out)
    coarse_copy.start()
    loss_out[...] = loss_round(4, None, None)
    mine_copy = pltpu.make_async_copy(heads.at[core], heads_out.at[core], local_sem.at[2])
    for d in (1, 3, 2):
        for q, (first, _, _) in enumerate(ORDERS):
            copies.wait(f"spread{q}{d}")
            got = (heads, core, q, (place[first] + 4 - d) % 4)
            copies.start(f"share{q}{d}", got, got, here.sibling)
    mine_copy.start()
    copies.wait(*[f"share{q}{d}" for q in range(3) for d in range(4)])
    other_copy = pltpu.make_async_copy(heads.at[other], heads_out.at[other], local_sem.at[3])
    other_copy.start()
    copies.finish()
    fine_copy.wait()
    coarse_copy.wait()
    mine_copy.wait()
    other_copy.wait()


def place_results(pairs, loss_in, fine_in, coarse_in, heads, loss, fine_grad, coarse_grad, fine_head_grad, coarse_head_grad):
    loss[0] = jnp.sum(loss_in[...]) * (1.0 / pairs)
    fine_grad[...] = fine_in[...]
    coarse_grad[...] = coarse_in[...]
    halves, parts, bands, pieces, _, n, lanes = heads.shape
    for side in range(halves):
        for q in range(parts):
            cols = pl.ds((side * parts + q) * lanes, lanes)
            for k in range(bands):
                for j in range(pieces):
                    at = pl.ds((k * pieces + j) * n, n)
                    fine_head_grad[at, cols] = heads[side, q, k, j, 0].astype(F32)
                    coarse_head_grad[at, cols] = heads[side, q, k, j, 1].astype(F32)


def shards(fine_rows, coarse_rows, fine_head, coarse_head, log_scale, bias):
    rows, width = fine_rows.shape
    wide, n = width // 2, rows // 4
    vmem = pl.BlockSpec(memory_space=pltpu.VMEM)
    smem = pl.BlockSpec(memory_space=pltpu.SMEM)
    anywhere = pl.BlockSpec(memory_space=pl.ANY)
    scratch = [
        VMEM((4, 4 * rows, width), BF16),
        VMEM((2, 4 * rows, width), BF16),
        VMEM((4, 4 * rows, width), F32),
        VMEM((2, 4 * rows, width), F32),
        VMEM((2, rows, width), F32),
        VMEM((2, 5 * rows, 1), F32),
        VMEM((2, 5 * rows, width), BF16),
        VMEM((2, 8, width), F32),
        VMEM((8, width), F32),
        VMEM((4 * rows, width), BF16),
        VMEM((2, 4 * rows, width), BF16),
        VMEM((2, rows, width), BF16),
        VMEM((4, rows, width), BF16),
        VMEM((2, 2, rows, width), BF16),
        VMEM((4, 2, rows, width), BF16),
        VMEM((2, rows, width), BF16),
        VMEM((2, rows, width), BF16),
        VMEM((2, rows, width), F32),
        VMEM((2, 2, 5 * rows, wide), BF16),
        VMEM((2, width, wide), BF16),
        VMEM((2, width, wide), BF16),
        VMEM((3, 4, 2, rows, 128), BF16),
        VMEM((3, 3, 2, rows, 128), BF16),
        VMEM((3, 4, 2, n, 128), BF16),
        VMEM((3, 3, 2, n, 128), BF16),
        VMEM((3, 4, 2, n, 128), BF16),
        VMEM((2, 3, 4, 4, 2, n, 128), BF16),
        VMEM((4, 4, 8, 128), F32),
        pltpu.SemaphoreType.DMA((N_COPIES,)),
        pltpu.SemaphoreType.DMA((N_COPIES,)),
        pltpu.SemaphoreType.DMA((4,)),
    ]
    tokens = rows * lax.axis_size("grp") * lax.axis_size("mem")
    pair_flops = 6 * (16 * rows) * (8 * rows) * width
    grad = jax.ShapeDtypeStruct((rows, width), F32)
    head = jax.ShapeDtypeStruct((width, width), F32)
    loss, fine_grad, coarse_grad, heads = pl.pallas_call(
        kernel,
        out_shape=(
            jax.ShapeDtypeStruct((8, 128), F32),
            grad,
            grad,
            jax.ShapeDtypeStruct((2, 3, 4, 4, 2, n, 128), BF16),
        ),
        in_specs=[vmem, vmem, vmem, vmem, smem, smem],
        out_specs=(vmem, anywhere, anywhere, anywhere),
        scratch_shapes=scratch,
        cost_estimate=pl.CostEstimate(flops=pair_flops, bytes_accessed=tokens * width, transcendentals=0),
        compiler_params=pltpu.CompilerParams(collective_id=0, has_side_effects=True, vmem_limit_bytes=60 * 2**20),
    )(fine_rows, coarse_rows, fine_head, coarse_head, log_scale, bias)

    def place(*refs):
        place_results(float(tokens) ** 2, *refs)

    by_rows = pl.BlockSpec((rows * 2, width), lambda i: (i, 0))
    by_halves = pl.BlockSpec((rows // 2, width), lambda i: (i, 0))
    return pl.pallas_call(
        place,
        grid=(2,),
        out_shape=(jax.ShapeDtypeStruct((1,), F32), grad, grad, head, head),
        in_specs=[
            pl.BlockSpec((8, 128), lambda i: (0, 0)),
            by_halves,
            by_halves,
            pl.BlockSpec((2, 3, 2, 4, 2, n, 128), lambda i: (0, 0, i, 0, 0, 0, 0)),
        ],
        out_specs=(smem, by_halves, by_halves, by_rows, by_rows),
    )(loss, fine_grad, coarse_grad, heads)


def solution(mesh):
    placed = (P(("grp", "mem"), None), P(("grp", "mem"), None), P(), P(), P(), P())
    return jax.shard_map(
        shards,
        mesh=mesh,
        in_specs=placed,
        out_specs=(P(), P(("grp", "mem"), None), P(("grp", "mem"), None), P(), P()),
        check_vma=False,
    )
```

```python
import jax
import jax.numpy as jnp
from jax import lax
from jax.experimental import pallas as pl
from jax.experimental.pallas import tpu as pltpu
from jax.sharding import PartitionSpec as P

MESH = pl.DeviceIdType.MESH
EPS = 1e-06
F32 = jnp.float32
BF16 = jnp.bfloat16
VMEM = pltpu.VMEM


def dot(a, b, dims):
    return lax.dot_general(a, b, (dims, ((), ())), preferred_element_type=F32)


NN = ((1,), (0,))
NT = ((1,), (1,))
TN = ((0,), (0,))


class Place:
    def __init__(self):
        grp, mem = lax.axis_index("grp"), lax.axis_index("mem")
        self.core = mem % 2
        self.x, self.y = (mem // 2) % 4, grp % 4
        self.z = (mem // 8) * 2 + grp // 4
        self.steps = {("x", d): self.at(dx=d) for d in (1, 2, 3)}
        self.steps |= {("y", d): self.at(dy=d) for d in (1, 2, 3)}
        self.steps |= {("z", d): self.at(z=(self.z + d) % 4) for d in (1, 2, 3)}
        self.sibling = self.at(core=1 - self.core)
        self.other_hi = self.steps["z", 2]
        self.other_lo = self.at(z=self.z + 1 - 2 * (self.z % 2))

    def at(self, dx=0, dy=0, z=None, core=None):
        x, y = (self.x + dx) % 4, (self.y + dy) % 4
        z = self.z if z is None else z
        core = self.core if core is None else core
        return ((z % 2) * 4 + y, (z // 2) * 8 + x * 2 + core)

    def along(self, axis, step):
        return self.steps[axis, step]


def view(ref, *index):
    return ref.at[index] if index else ref


class Copies:
    def __init__(self, send_sem, recv_sem):
        self.send_sem, self.recv_sem = send_sem, recv_sem
        self.made, self.sent = {}, set()

    def start(self, name, src, dst, device):
        index = len(self.made)
        assert name not in self.made and index < N_COPIES

        def make():
            return pltpu.make_async_remote_copy(
                src_ref=view(*src),
                dst_ref=view(*dst),
                send_sem=self.send_sem.at[index],
                recv_sem=self.recv_sem.at[index],
                device_id=device,
                device_id_type=MESH,
            )

        self.made[name] = make
        make().start()

    def wait(self, *names):
        for name in names:
            self.made[name]().wait_recv()

    def leave(self, *names):
        for name in names:
            self.sent.add(name)
            self.made[name]().wait_send()

    def finish(self):
        self.leave(*[name for name in self.made if name not in self.sent])


N_COPIES = 144
ORDERS = (("x", "y", "z"), ("y", "z", "x"), ("z", "x", "y"))


def kernel(
    fine_rows,
    coarse_rows,
    fine_head,
    coarse_head,
    log_scale,
    bias,
    loss_out,
    fine_grad_out,
    coarse_grad_out,
    heads_out,
    fine_all,
    coarse_all,
    fine_acc,
    coarse_acc,
    unit_keep,
    inv_keep,
    rows_keep,
    consts,
    loss_acc,
    sib_out,
    sib_in,
    half_out,
    half_in,
    full_out,
    full_in,
    hop_out,
    hop_in,
    own_sum,
    dp_keep,
    share_out,
    share_in,
    part_out,
    part_in,
    quarter_out,
    quarter_in,
    column,
    heads,
    loss_parts,
    send_sem,
    recv_sem,
    local_sem,
):
    rows, width = fine_rows.shape
    half = rows // 2
    wide = width // 2
    here = Place()
    copies = Copies(send_sem, recv_sem)
    upper, lower = pl.ds(0, half), pl.ds(half, half)

    def slot(step):
        return pl.ds((step % 4) * rows, rows)

    def slot_half(step, which):
        return pl.ds((step % 4) * rows + which * half, half)

    barrier = pltpu.get_barrier_semaphore()
    partners = [here.sibling]
    partners += [here.along(axis, step) for axis in "xyz" for step in (1, 2, 3)]
    for device in partners:
        pl.semaphore_signal(barrier, inc=1, device_id=device, device_id_type=MESH)

    consts[0] = 0.5 * jnp.exp(jnp.full((8, width), log_scale[0], F32))
    consts[1] = jnp.full((8, width), 0.5 * bias[0], F32)
    h, shift = consts[0, 0:1, :], consts[1, 0:1, :]
    inputs = (fine_rows, coarse_rows)

    far_rows = 4 * rows

    def embed(which, start, keep_unit=False):
        at = pl.ds(start, rows)
        proj = dot(rows_keep[which, at], (fine_head, coarse_head)[which][...], NN)
        inv = lax.rsqrt(jnp.sum(proj * proj, axis=-1, keepdims=True) + EPS)
        unit = proj * inv
        if keep_unit:
            unit_keep[which] = unit
        inv_keep[which, at] = inv
        return unit.astype(BF16)

    rows_keep[0, slot(0)] = fine_rows[...]
    rows_keep[1, pl.ds(far_rows, rows)] = coarse_rows[...]
    pl.semaphore_wait(barrier, len(partners))
    far_device = (here.other_hi, here.other_lo)

    def to_far(which, start, end):
        for p in (0, 1):
            copies.start(
                f"z{which}{p}",
                (rows_keep, which, pl.ds(start + p * half, half)),
                (rows_keep, which, pl.ds(end + p * half, half)),
                far_device[which],
            )

    def send_both(tag, axis, buf, at, order_plus, order_minus):
        for p in order_plus:
            copies.start(f"{tag}+{p}", (buf, at, slot_half(0, p)), (buf, at, slot_half(-1, p)), here.along(axis, 1))
        for p in order_minus:
            copies.start(f"{tag}-{p}", (buf, at, slot_half(0, p)), (buf, at, slot_half(1, p)), here.along(axis, 3))

    def pass_plus(tag, axis, buf, at):
        copies.wait(tag + "+0")
        copies.start(tag + "++", (buf, at, slot_half(-1, 0)), (buf, at, slot_half(2, 0)), here.along(axis, 1))

    def pass_minus(tag, axis, buf, at):
        copies.wait(tag + "-1")
        copies.start(tag + "--", (buf, at, slot_half(1, 1)), (buf, at, slot_half(2, 1)), here.along(axis, 3))

    def sib_near(tag, at):
        copies.wait(tag + "+1")
        copies.start(tag + "+s", (fine_all, at, slot(-1)), (fine_all, at + 1, slot(-1)), here.sibling)
        copies.wait(tag + "-0")
        copies.start(tag + "-s", (fine_all, at, slot(1)), (fine_all, at + 1, slot(1)), here.sibling)

    def sib_far(tag, at):
        copies.wait(tag + "++", tag + "--")
        copies.start(tag + "2s", (fine_all, at, slot(2)), (fine_all, at + 1, slot(2)), here.sibling)

    to_far(0, 0, far_rows)
    send_both("fx", "x", rows_keep, 0, (0, 1), (1, 0))
    to_far(1, far_rows, 0)
    coarse_all[0, slot(0)] = embed(1, far_rows, True)
    send_both("cy", "y", coarse_all, 0, (0, 1), (1, 0))
    fine_all[0, slot(0)] = embed(0, 0, True)
    copies.start("fs", (fine_all, 0, slot(0)), (fine_all, 1, slot(0)), here.sibling)

    coarse_acc[...] = jnp.zeros_like(coarse_acc)
    fine_acc[...] = jnp.zeros_like(fine_acc)
    loss_acc[...] = jnp.zeros_like(loss_acc)

    fine_emb = fine_all[0, slot(0)].astype(F32)
    coarse_emb = coarse_all[0, slot(0)].astype(F32)
    arg = jnp.sum(fine_emb * coarse_emb, axis=-1, keepdims=True) * consts[0, 0:1, 0:1] + consts[1, 0:1, 0:1]
    tanh = jnp.tanh(arg)
    delta = (tanh - 1.0).astype(BF16).astype(F32) - (1.0 + tanh).astype(BF16).astype(F32)
    own_sum[0] = delta * coarse_emb
    own_sum[1] = delta * fine_emb
    diagonal = jnp.sum(2.0 * arg, axis=0, keepdims=True)

    pass_plus("fx", "x", rows_keep, 0)
    pass_minus("fx", "x", rows_keep, 0)
    pass_plus("cy", "y", coarse_all, 0)
    pass_minus("cy", "y", coarse_all, 0)

    def near_fine(step, name):
        fine_all[0, slot(step)] = embed(0, (step % 4) * rows)
        copies.start(name, (fine_all, 0, slot(step)), (fine_all, 1, slot(step)), here.sibling)

    copies.wait("z00", "z01")
    fine_all[2, slot(0)] = embed(0, far_rows)
    send_both("gx", "x", fine_all, 2, (0, 1), (1, 0))
    copies.wait("fx+1")
    near_fine(-1, "fx+s")
    copies.wait("fx-0")
    near_fine(1, "fx-s")
    copies.start("gs", (fine_all, 2, slot(0)), (fine_all, 3, slot(0)), here.sibling)
    copies.wait("fx++", "fx--")
    near_fine(2, "fx2s")
    copies.wait("cy+1", "cy-0", "cy++", "cy--")

    def far_coarse(step):
        coarse_all[1, slot(step)] = embed(1, (step % 4) * rows)

    def tile(fg, cg):
        cols = coarse_all[cg]
        n = 2 * rows
        coefs = []
        for j in range(4 * rows // n):
            at = pl.ds(j * n, n)
            t = jnp.tanh(dot(fine_all[fg, at], cols, NT) * h + shift)
            coef = (1.0 + t).astype(BF16)
            rest = 1.0 - t
            eighth = n // 8
            p = [rest[i * eighth : (i + 1) * eighth] for i in range(8)]
            p = ((p[0] * p[1]) * (p[2] * p[3])) * ((p[4] * p[5]) * (p[6] * p[7]))
            p = jnp.log(p * (1.0 / 256.0))
            for i in range(0, eighth, 8):
                loss_acc[...] -= p[i : i + 8]
            fine_acc[fg, at] += dot(coef, cols, NN)
            coefs.append(coef)
        coarse_acc[cg] += dot(jnp.concatenate(coefs, 0), fine_all[fg], TN)

    def to_sibling(k):
        if k == 0:
            copies.leave("sum_s1")
        sib_out[...] = fine_acc[2 * k + 1].astype(BF16)
        copies.start(f"sum_s{k}", (sib_out,), (sib_in, k), here.sibling)

    def ring_start(tag, axis, r, acc, a, other):
        def total(step, p):
            value = acc[a, slot_half(step, p)]
            return value if other is None else value + sib_in[other, slot_half(step, p)].astype(F32)

        if r % 2 == 0:
            earlier = {0: "f1", 2: "c0"}[r]
            copies.leave(*[earlier + name for name in ("h+", "h-", "f+0", "f+1", "f-0", "f-1")])
        plus, minus = here.along(axis, 1), here.along(axis, 3)
        half_out[r // 2, upper] = total(2, 0).astype(BF16)
        copies.start(tag + "h+", (half_out, r // 2, upper), (half_in, r, upper), plus)
        half_out[r // 2, lower] = total(2, 1).astype(BF16)
        copies.start(tag + "h-", (half_out, r // 2, lower), (half_in, r, lower), minus)
        full_out[r // 2, 0, lower] = total(1, 1).astype(BF16)
        copies.start(tag + "f+1", (full_out, r // 2, 0, lower), (full_in, r, 0, lower), plus)
        full_out[r // 2, 1, upper] = total(3, 0).astype(BF16)
        copies.start(tag + "f-0", (full_out, r // 2, 1, upper), (full_in, r, 1, upper), minus)

    def ring_own(acc, a, other):
        for step, p in ((1, 0), (3, 1), (0, 0), (0, 1)):
            at = slot_half(step, p)
            acc[a, at] += sib_in[other, at].astype(F32)

    def ring_middle(tag, axis, r, acc, a):
        copies.wait(tag + "h+")
        full_out[r // 2, 0, upper] = (acc[a, slot_half(1, 0)] + half_in[r, upper].astype(F32)).astype(BF16)
        copies.start(tag + "f+0", (full_out, r // 2, 0, upper), (full_in, r, 0, upper), here.along(axis, 1))
        copies.wait(tag + "h-")
        full_out[r // 2, 1, lower] = (acc[a, slot_half(3, 1)] + half_in[r, lower].astype(F32)).astype(BF16)
        copies.start(tag + "f-1", (full_out, r // 2, 1, lower), (full_in, r, 1, lower), here.along(axis, 3))

    def ring_end(tag, r, acc, a):
        copies.wait(tag + "f+0", tag + "f+1", tag + "f-0", tag + "f-1")
        return acc[a, slot(0)] + full_in[r, 0].astype(F32) + full_in[r, 1].astype(F32)

    def hop(which, *parts):
        for p in parts:
            at = pl.ds(p * half, half)
            copies.start(f"hop{which}{p}", (hop_out, which, at), (hop_in, which, at), far_device[which])

    def step(t, carry):
        @pl.when(t == 1)
        def _():
            pass_plus("gx", "x", fine_all, 2)
            pass_minus("gx", "x", fine_all, 2)
            copies.wait("z10", "z11")
            send_both("dy", "y", rows_keep, 1, (0, 1), (1, 0))
            copies.wait("fs", "fx+s", "fx-s", "fx2s")

        @pl.when(t == 2)
        def _():
            sib_near("gx", 2)
            far_coarse(0)
            sib_far("gx", 2)
            pass_plus("dy", "y", rows_keep, 1)
            pass_minus("dy", "y", rows_keep, 1)

        @pl.when(t == 3)
        def _():
            copies.wait("gs", "gx+s", "gx-s", "gx2s", "dy+1", "dy-0")
            far_coarse(-1)
            far_coarse(1)

        @pl.when(t == 4)
        def _():
            ring_start("c0", "y", 3, coarse_acc, 0, None)
            copies.wait("dy++", "dy--")
            far_coarse(2)

        @pl.when(t == 5)
        def _():
            to_sibling(1)

        @pl.when(t == 6)
        def _():
            copies.wait("sum_s1")
            ring_start("f1", "x", 1, fine_acc, 2, 1)
            ring_own(fine_acc, 2, 1)
            ring_middle("c0", "y", 3, coarse_acc, 0)

        @pl.when(t == 7)
        def _():
            to_sibling(0)
            ring_middle("f1", "x", 1, fine_acc, 2)

        late = t // 4
        tile(t + late * (7 - 2 * t), late)
        return carry

    lax.fori_loop(0, 8, step, 0)

    def back(value, unit, inv):
        inner = jnp.sum(unit * value, axis=-1, keepdims=True)
        return ((inv * h) * (value - unit * inner)).astype(BF16)

    def keep(which, start, value_at, buf, a, first):
        n = 32
        for i in range(0, rows, n):
            at = pl.ds(start + i, n)
            dp = back(value_at(i, n), buf[a, pl.ds(first + i, n)].astype(F32), inv_keep[which, at])
            for side in (0, 1):
                dp_keep[which, side, at] = dp[:, side * wide : (side + 1) * wide]

    def grad_to_out(which, start, value, head_ref, out):
        dp = back(value, unit_keep[which], inv_keep[which, pl.ds(start, rows)])
        fine_acc[2 * which + 1, slot(0)] = dot(dp, head_ref[...], NT)
        return pltpu.make_async_copy(fine_acc.at[2 * which + 1, slot(0)], out, local_sem.at[which])

    core = here.core
    other = 1 - core

    ring_start("c1", "y", 2, coarse_acc, 1, None)
    copies.wait("sum_s0")
    for i in range(4):
        fine_acc[0, slot(i)] += sib_in[0, slot(i)].astype(F32)
    ring_start("f0", "x", 0, fine_acc, 0, None)
    own_sum[1] += ring_end("c0", 3, coarse_acc, 0)
    keep(1, far_rows, lambda i, n: own_sum[1, pl.ds(i, n)], coarse_all, 0, 0)
    keep(1, 0, lambda i, n: coarse_acc[1, pl.ds(i, n)], coarse_all, 1, 0)
    keep(1, rows, lambda i, n: coarse_acc[1, pl.ds(rows + i, n)], coarse_all, 1, rows)
    keep(1, 2 * rows, lambda i, n: coarse_acc[1, pl.ds(2 * rows + i, n)], coarse_all, 1, 2 * rows)
    keep(1, 3 * rows, lambda i, n: coarse_acc[1, pl.ds(3 * rows + i, n)], coarse_all, 1, 3 * rows)
    value = ring_end("f1", 1, fine_acc, 2)
    hop_out[0] = value.astype(BF16)
    fine_acc[2, slot(0)] = value
    hop(0, 0, 1)
    share_out[1] = dot(rows_keep[1], dp_keep[1, other], TN).astype(BF16)
    keep(0, 0, lambda i, n: fine_acc[0, pl.ds(i, n)] + own_sum[0, pl.ds(i, n)], fine_all, 0, 0)
    keep(0, rows, lambda i, n: fine_acc[0, pl.ds(rows + i, n)], fine_all, 0, rows)
    keep(0, 2 * rows, lambda i, n: fine_acc[0, pl.ds(2 * rows + i, n)], fine_all, 0, 2 * rows)
    keep(0, 3 * rows, lambda i, n: fine_acc[0, pl.ds(3 * rows + i, n)], fine_all, 0, 3 * rows)
    copies.start("part_s1", (share_out, 1), (share_in, 1), here.sibling)
    ring_middle("c1", "y", 2, coarse_acc, 1)
    keep(0, far_rows, lambda i, n: fine_acc[2, pl.ds(i, n)], fine_all, 2, 0)
    share_out[0] = dot(rows_keep[0], dp_keep[0, other], TN).astype(BF16)
    copies.start("part_s0", (share_out, 0), (share_in, 0), here.sibling)

    loss = loss_acc[:, 0:128]
    for i in range(1, width // 128):
        loss = loss + loss_acc[:, i * 128 : (i + 1) * 128]
    at_origin = (lax.broadcasted_iota(jnp.int32, (8, 128), 0) + lax.broadcasted_iota(jnp.int32, (8, 128), 1)) == 0
    loss = loss - jnp.where(at_origin, diagonal, 0.0)
    loss_parts[0, 0] = loss
    copies.start("loss_s", (loss_parts, 0, 0), (loss_parts, 0, 1), here.sibling)

    def loss_round(r, axis, place):
        if r == 1:
            copies.wait("loss_s")
            value = loss_parts[0, 0] + loss_parts[0, 1]
        else:
            copies.wait(*[f"loss{r - 1}{d}" for d in (1, 2, 3)])
            q = loss_parts
            value = (q[r - 1, 0] + q[r - 1, 1]) + (q[r - 1, 2] + q[r - 1, 3])
        if axis is None:
            return value
        loss_parts[r, place] = value
        for d in (1, 2, 3):
            copies.start(f"loss{r}{d}", (loss_parts, r, place), (loss_parts, r, place), here.along(axis, d))

    place = {"x": here.x, "y": here.y, "z": here.z}
    n = rows // 4
    for which in (1, 0):
        value = dot(rows_keep[which], dp_keep[which, core], TN)
        copies.wait(f"part_s{which}")
        value = value + share_in[which].astype(F32)
        for q in range(3):
            for j in range(4):
                part_out[q, j, which] = value[j * rows : (j + 1) * rows, q * 128 : (q + 1) * 128].astype(BF16)
    for d in (1, 3, 2):
        for q, (first, _, _) in enumerate(ORDERS):
            copies.start(f"part{q}{d}", (part_out, q, (place[first] + d) % 4), (part_in, q, d - 1), here.along(first, d))

    loss_round(1, "x", here.x)

    for q, (first, second, _) in enumerate(ORDERS):
        copies.wait(*[f"part{q}{d}" for d in (1, 2, 3)])
        value = part_out[q, place[first]].astype(F32)
        for d in range(3):
            value = value + part_in[q, d].astype(F32)
        for j in range(4):
            quarter_out[q, j] = value[:, j * n : (j + 1) * n].astype(BF16)
        for d in (1, 3, 2):
            copies.start(f"quarter{q}{d}", (quarter_out, q, (place[second] + d) % 4), (quarter_in, q, d - 1), here.along(second, d))
    loss_round(2, "y", here.y)
    hop_out[1] = ring_end("c1", 2, coarse_acc, 1).astype(BF16)
    hop(1, 0)
    ring_middle("f0", "x", 0, fine_acc, 0)
    for q, (_, second, third) in enumerate(ORDERS):
        copies.wait(*[f"quarter{q}{d}" for d in (1, 2, 3)])
        value = quarter_out[q, place[second]].astype(F32)
        for d in range(3):
            value = value + quarter_in[q, d].astype(F32)
        column[q, place[third]] = value.astype(BF16)
        mine = (column, q, place[third])
        for d in (1, 3, 2):
            copies.start(f"column{q}{d}", mine, mine, here.along(third, d))
    hop(1, 1)
    loss_round(3, "z", here.z)
    for q, (first, second, third) in enumerate(ORDERS):
        copies.wait(*[f"column{q}{d}" for d in (1, 2, 3)])
        value = column[q, 0].astype(F32)
        for i in range(1, 4):
            value = value + column[q, i].astype(F32)
        heads[core, q, place[first], place[second]] = value.astype(BF16)
        mine = (heads, core, q, place[first], place[second])
        for d in (1, 3, 2):
            copies.start(f"back{q}{d}", mine, mine, here.along(second, d))
    own_sum[0] += ring_end("f0", 0, fine_acc, 0)
    copies.wait("hop00", "hop01")
    fine_copy = grad_to_out(0, 0, own_sum[0] + hop_in[0].astype(F32), fine_head, fine_grad_out)
    fine_copy.start()
    for q, (first, second, _) in enumerate(ORDERS):
        copies.wait(*[f"back{q}{d}" for d in (1, 2, 3)])
        mine = (heads, core, q, place[first])
        for d in (1, 3, 2):
            copies.start(f"spread{q}{d}", mine, mine, here.along(first, d))
    for q, (first, _, _) in enumerate(ORDERS):
        mine = (heads, core, q, place[first])
        copies.start(f"share{q}0", mine, mine, here.sibling)
    copies.wait("hop10", "hop11")
    coarse_copy = grad_to_out(1, far_rows, own_sum[1] + hop_in[1].astype(F32), coarse_head, coarse_grad_out)
    coarse_copy.start()
    loss_out[...] = loss_round(4, None, None)
    mine_copy = pltpu.make_async_copy(heads.at[core], heads_out.at[core], local_sem.at[2])
    for d in (1, 3, 2):
        for q, (first, _, _) in enumerate(ORDERS):
            copies.wait(f"spread{q}{d}")
            got = (heads, core, q, (place[first] + 4 - d) % 4)
            copies.start(f"share{q}{d}", got, got, here.sibling)
    mine_copy.start()
    copies.wait(*[f"share{q}{d}" for q in range(3) for d in range(4)])
    other_copy = pltpu.make_async_copy(heads.at[other], heads_out.at[other], local_sem.at[3])
    other_copy.start()
    copies.finish()
    fine_copy.wait()
    coarse_copy.wait()
    mine_copy.wait()
    other_copy.wait()


def place_results(pairs, loss_in, fine_in, coarse_in, heads, loss, fine_grad, coarse_grad, fine_head_grad, coarse_head_grad):
    loss[0] = jnp.sum(loss_in[...]) * (1.0 / pairs)
    fine_grad[...] = fine_in[...]
    coarse_grad[...] = coarse_in[...]
    halves, parts, bands, pieces, _, n, lanes = heads.shape
    for side in range(halves):
        for q in range(parts):
            cols = pl.ds((side * parts + q) * lanes, lanes)
            for k in range(bands):
                for j in range(pieces):
                    at = pl.ds((k * pieces + j) * n, n)
                    fine_head_grad[at, cols] = heads[side, q, k, j, 0].astype(F32)
                    coarse_head_grad[at, cols] = heads[side, q, k, j, 1].astype(F32)


def shards(fine_rows, coarse_rows, fine_head, coarse_head, log_scale, bias):
    rows, width = fine_rows.shape
    wide, n = width // 2, rows // 4
    vmem = pl.BlockSpec(memory_space=pltpu.VMEM)
    smem = pl.BlockSpec(memory_space=pltpu.SMEM)
    anywhere = pl.BlockSpec(memory_space=pl.ANY)
    scratch = [
        VMEM((4, 4 * rows, width), BF16),
        VMEM((2, 4 * rows, width), BF16),
        VMEM((4, 4 * rows, width), F32),
        VMEM((2, 4 * rows, width), F32),
        VMEM((2, rows, width), F32),
        VMEM((2, 5 * rows, 1), F32),
        VMEM((2, 5 * rows, width), BF16),
        VMEM((2, 8, width), F32),
        VMEM((8, width), F32),
        VMEM((4 * rows, width), BF16),
        VMEM((2, 4 * rows, width), BF16),
        VMEM((2, rows, width), BF16),
        VMEM((4, rows, width), BF16),
        VMEM((2, 2, rows, width), BF16),
        VMEM((4, 2, rows, width), BF16),
        VMEM((2, rows, width), BF16),
        VMEM((2, rows, width), BF16),
        VMEM((2, rows, width), F32),
        VMEM((2, 2, 5 * rows, wide), BF16),
        VMEM((2, width, wide), BF16),
        VMEM((2, width, wide), BF16),
        VMEM((3, 4, 2, rows, 128), BF16),
        VMEM((3, 3, 2, rows, 128), BF16),
        VMEM((3, 4, 2, n, 128), BF16),
        VMEM((3, 3, 2, n, 128), BF16),
        VMEM((3, 4, 2, n, 128), BF16),
        VMEM((2, 3, 4, 4, 2, n, 128), BF16),
        VMEM((4, 4, 8, 128), F32),
        pltpu.SemaphoreType.DMA((N_COPIES,)),
        pltpu.SemaphoreType.DMA((N_COPIES,)),
        pltpu.SemaphoreType.DMA((4,)),
    ]
    tokens = rows * lax.axis_size("grp") * lax.axis_size("mem")
    pair_flops = 6 * (16 * rows) * (8 * rows) * width
    grad = jax.ShapeDtypeStruct((rows, width), F32)
    head = jax.ShapeDtypeStruct((width, width), F32)
    loss, fine_grad, coarse_grad, heads = pl.pallas_call(
        kernel,
        out_shape=(
            jax.ShapeDtypeStruct((8, 128), F32),
            grad,
            grad,
            jax.ShapeDtypeStruct((2, 3, 4, 4, 2, n, 128), BF16),
        ),
        in_specs=[vmem, vmem, vmem, vmem, smem, smem],
        out_specs=(vmem, anywhere, anywhere, anywhere),
        scratch_shapes=scratch,
        cost_estimate=pl.CostEstimate(flops=pair_flops, bytes_accessed=tokens * width, transcendentals=0),
        compiler_params=pltpu.CompilerParams(collective_id=0, has_side_effects=True, vmem_limit_bytes=60 * 2**20),
    )(fine_rows, coarse_rows, fine_head, coarse_head, log_scale, bias)

    def place(*refs):
        place_results(float(tokens) ** 2, *refs)

    by_rows = pl.BlockSpec((rows * 2, width), lambda i: (i, 0))
    by_halves = pl.BlockSpec((rows // 2, width), lambda i: (i, 0))
    return pl.pallas_call(
        place,
        grid=(2,),
        out_shape=(jax.ShapeDtypeStruct((1,), F32), grad, grad, head, head),
        in_specs=[
            pl.BlockSpec((8, 128), lambda i: (0, 0)),
            by_halves,
            by_halves,
            pl.BlockSpec((2, 3, 2, 4, 2, n, 128), lambda i: (0, 0, i, 0, 0, 0, 0)),
        ],
        out_specs=(smem, by_halves, by_halves, by_rows, by_rows),
    )(loss, fine_grad, coarse_grad, heads)


def solution(mesh):
    placed = (P(("grp", "mem"), None), P(("grp", "mem"), None), P(), P(), P(), P())
    return jax.shard_map(
        shards,
        mesh=mesh,
        in_specs=placed,
        out_specs=(P(), P(("grp", "mem"), None), P(("grp", "mem"), None), P(), P()),
        check_vma=False,
    )
```

```python
import jax
import jax.numpy as jnp
from jax import lax
from jax.experimental import pallas as pl
from jax.experimental.pallas import tpu as pltpu
from jax.sharding import PartitionSpec as P

MESH = pl.DeviceIdType.MESH
EPS = 1e-06
F32 = jnp.float32
BF16 = jnp.bfloat16
VMEM = pltpu.VMEM


def dot(a, b, dims):
    return lax.dot_general(a, b, (dims, ((), ())), preferred_element_type=F32)


NN = ((1,), (0,))
NT = ((1,), (1,))
TN = ((0,), (0,))


class Place:
    def __init__(self):
        grp, mem = lax.axis_index("grp"), lax.axis_index("mem")
        self.core = mem % 2
        self.x, self.y = (mem // 2) % 4, grp % 4
        self.z = (mem // 8) * 2 + grp // 4
        self.steps = {("x", d): self.at(dx=d) for d in (1, 2, 3)}
        self.steps |= {("y", d): self.at(dy=d) for d in (1, 2, 3)}
        self.steps |= {("z", d): self.at(z=(self.z + d) % 4) for d in (1, 2, 3)}
        self.sibling = self.at(core=1 - self.core)
        self.other_hi = self.steps["z", 2]
        self.other_lo = self.at(z=self.z + 1 - 2 * (self.z % 2))

    def at(self, dx=0, dy=0, z=None, core=None):
        x, y = (self.x + dx) % 4, (self.y + dy) % 4
        z = self.z if z is None else z
        core = self.core if core is None else core
        return ((z % 2) * 4 + y, (z // 2) * 8 + x * 2 + core)

    def along(self, axis, step):
        return self.steps[axis, step]


def view(ref, *index):
    return ref.at[index] if index else ref


class Copies:
    def __init__(self, send_sem, recv_sem):
        self.send_sem, self.recv_sem = send_sem, recv_sem
        self.made, self.sent = {}, set()

    def start(self, name, src, dst, device):
        index = len(self.made)
        assert name not in self.made and index < N_COPIES

        def make():
            return pltpu.make_async_remote_copy(
                src_ref=view(*src),
                dst_ref=view(*dst),
                send_sem=self.send_sem.at[index],
                recv_sem=self.recv_sem.at[index],
                device_id=device,
                device_id_type=MESH,
            )

        self.made[name] = make
        make().start()

    def wait(self, *names):
        for name in names:
            self.made[name]().wait_recv()

    def leave(self, *names):
        for name in names:
            self.sent.add(name)
            self.made[name]().wait_send()

    def finish(self):
        self.leave(*[name for name in self.made if name not in self.sent])


N_COPIES = 144
ORDERS = (("x", "y", "z"), ("y", "z", "x"), ("z", "x", "y"))


def kernel(
    fine_rows,
    coarse_rows,
    fine_head,
    coarse_head,
    log_scale,
    bias,
    loss_out,
    fine_grad_out,
    coarse_grad_out,
    heads_out,
    fine_all,
    coarse_all,
    fine_acc,
    coarse_acc,
    unit_keep,
    inv_keep,
    rows_keep,
    heads_in,
    consts,
    loss_acc,
    sib_out,
    sib_in,
    half_out,
    half_in,
    full_out,
    full_in,
    hop_out,
    hop_in,
    own_sum,
    dp_keep,
    share_out,
    share_in,
    part_out,
    part_in,
    quarter_out,
    quarter_in,
    column,
    heads,
    loss_parts,
    send_sem,
    recv_sem,
    local_sem,
):
    rows, width = fine_rows.shape
    half = rows // 2
    wide = width // 2
    here = Place()
    copies = Copies(send_sem, recv_sem)
    upper, lower = pl.ds(0, half), pl.ds(half, half)

    def slot(step):
        return pl.ds((step % 4) * rows, rows)

    def slot_half(step, which):
        return pl.ds((step % 4) * rows + which * half, half)

    barrier = pltpu.get_barrier_semaphore()
    partners = [here.sibling]
    partners += [here.along(axis, step) for axis in "xyz" for step in (1, 2, 3)]
    for device in partners:
        pl.semaphore_signal(barrier, inc=1, device_id=device, device_id_type=MESH)

    loads = [
        pltpu.make_async_copy(fine_rows, rows_keep.at[0, slot(0)], local_sem.at[4]),
        pltpu.make_async_copy(coarse_rows, rows_keep.at[1, pl.ds(4 * rows, rows)], local_sem.at[5]),
        pltpu.make_async_copy(coarse_head, heads_in.at[1], local_sem.at[6]),
        pltpu.make_async_copy(fine_head, heads_in.at[0], local_sem.at[7]),
    ]
    for load in loads:
        load.start()

    consts[0] = 0.5 * jnp.exp(jnp.full((8, width), log_scale[0], F32))
    consts[1] = jnp.full((8, width), 0.5 * bias[0], F32)
    h, shift = consts[0, 0:1, :], consts[1, 0:1, :]

    far_rows = 4 * rows

    def embed(which, start, keep_unit=False):
        at = pl.ds(start, rows)
        proj = dot(rows_keep[which, at], heads_in[which], NN)
        inv = lax.rsqrt(jnp.sum(proj * proj, axis=-1, keepdims=True) + EPS)
        unit = proj * inv
        if keep_unit:
            unit_keep[which] = unit
        inv_keep[which, at] = inv
        return unit.astype(BF16)

    for i in (0, 1):
        loads[i].wait()
    pl.semaphore_wait(barrier, len(partners))
    far_device = (here.other_hi, here.other_lo)

    def to_far(which, start, end):
        for p in (0, 1):
            copies.start(
                f"z{which}{p}",
                (rows_keep, which, pl.ds(start + p * half, half)),
                (rows_keep, which, pl.ds(end + p * half, half)),
                far_device[which],
            )

    def send_both(tag, axis, buf, at, order_plus, order_minus):
        for p in order_plus:
            copies.start(f"{tag}+{p}", (buf, at, slot_half(0, p)), (buf, at, slot_half(-1, p)), here.along(axis, 1))
        for p in order_minus:
            copies.start(f"{tag}-{p}", (buf, at, slot_half(0, p)), (buf, at, slot_half(1, p)), here.along(axis, 3))

    def pass_plus(tag, axis, buf, at):
        copies.wait(tag + "+0")
        copies.start(tag + "++", (buf, at, slot_half(-1, 0)), (buf, at, slot_half(2, 0)), here.along(axis, 1))

    def pass_minus(tag, axis, buf, at):
        copies.wait(tag + "-1")
        copies.start(tag + "--", (buf, at, slot_half(1, 1)), (buf, at, slot_half(2, 1)), here.along(axis, 3))

    def sib_near(tag, at):
        copies.wait(tag + "+1")
        copies.start(tag + "+s", (fine_all, at, slot(-1)), (fine_all, at + 1, slot(-1)), here.sibling)
        copies.wait(tag + "-0")
        copies.start(tag + "-s", (fine_all, at, slot(1)), (fine_all, at + 1, slot(1)), here.sibling)

    def sib_far(tag, at):
        copies.wait(tag + "++", tag + "--")
        copies.start(tag + "2s", (fine_all, at, slot(2)), (fine_all, at + 1, slot(2)), here.sibling)

    to_far(0, 0, far_rows)
    send_both("fx", "x", rows_keep, 0, (0, 1), (1, 0))
    to_far(1, far_rows, 0)
    loads[2].wait()
    coarse_all[0, slot(0)] = embed(1, far_rows, True)
    send_both("cy", "y", coarse_all, 0, (0, 1), (1, 0))
    loads[3].wait()
    fine_all[0, slot(0)] = embed(0, 0, True)
    copies.start("fs", (fine_all, 0, slot(0)), (fine_all, 1, slot(0)), here.sibling)

    coarse_acc[...] = jnp.zeros_like(coarse_acc)
    fine_acc[...] = jnp.zeros_like(fine_acc)
    loss_acc[...] = jnp.zeros_like(loss_acc)

    fine_emb = fine_all[0, slot(0)].astype(F32)
    coarse_emb = coarse_all[0, slot(0)].astype(F32)
    arg = jnp.sum(fine_emb * coarse_emb, axis=-1, keepdims=True) * consts[0, 0:1, 0:1] + consts[1, 0:1, 0:1]
    tanh = jnp.tanh(arg)
    delta = (tanh - 1.0).astype(BF16).astype(F32) - (1.0 + tanh).astype(BF16).astype(F32)
    own_sum[0] = delta * coarse_emb
    own_sum[1] = delta * fine_emb
    diagonal = jnp.sum(2.0 * arg, axis=0, keepdims=True)

    pass_plus("fx", "x", rows_keep, 0)
    pass_minus("fx", "x", rows_keep, 0)
    pass_plus("cy", "y", coarse_all, 0)
    pass_minus("cy", "y", coarse_all, 0)

    def near_fine(step, name):
        fine_all[0, slot(step)] = embed(0, (step % 4) * rows)
        copies.start(name, (fine_all, 0, slot(step)), (fine_all, 1, slot(step)), here.sibling)

    copies.wait("z00", "z01")
    fine_all[2, slot(0)] = embed(0, far_rows)
    send_both("gx", "x", fine_all, 2, (0, 1), (1, 0))
    copies.wait("fx+1")
    near_fine(-1, "fx+s")
    copies.wait("fx-0")
    near_fine(1, "fx-s")
    copies.start("gs", (fine_all, 2, slot(0)), (fine_all, 3, slot(0)), here.sibling)
    copies.wait("fx++", "fx--")
    near_fine(2, "fx2s")
    copies.wait("cy+1", "cy-0", "cy++", "cy--")

    def far_coarse(step):
        coarse_all[1, slot(step)] = embed(1, (step % 4) * rows)

    def tile(fg, cg):
        cols = coarse_all[cg]
        n = 2 * rows
        coefs = []
        for j in range(4 * rows // n):
            at = pl.ds(j * n, n)
            t = jnp.tanh(dot(fine_all[fg, at], cols, NT) * h + shift)
            coef = (1.0 + t).astype(BF16)
            rest = 1.0 - t
            eighth = n // 8
            p = [rest[i * eighth : (i + 1) * eighth] for i in range(8)]
            p = ((p[0] * p[1]) * (p[2] * p[3])) * ((p[4] * p[5]) * (p[6] * p[7]))
            p = jnp.log(p * (1.0 / 256.0))
            for i in range(0, eighth, 8):
                loss_acc[...] -= p[i : i + 8]
            fine_acc[fg, at] += dot(coef, cols, NN)
            coefs.append(coef)
        coarse_acc[cg] += dot(jnp.concatenate(coefs, 0), fine_all[fg], TN)

    def to_sibling(k):
        if k == 0:
            copies.leave("sum_s1")
        sib_out[...] = fine_acc[2 * k + 1].astype(BF16)
        copies.start(f"sum_s{k}", (sib_out,), (sib_in, k), here.sibling)

    def ring_start(tag, axis, r, acc, a, other):
        def total(step, p):
            value = acc[a, slot_half(step, p)]
            return value if other is None else value + sib_in[other, slot_half(step, p)].astype(F32)

        if r % 2 == 0:
            earlier = {0: "f1", 2: "c0"}[r]
            copies.leave(*[earlier + name for name in ("h+", "h-", "f+0", "f+1", "f-0", "f-1")])
        plus, minus = here.along(axis, 1), here.along(axis, 3)
        half_out[r // 2, upper] = total(2, 0).astype(BF16)
        copies.start(tag + "h+", (half_out, r // 2, upper), (half_in, r, upper), plus)
        half_out[r // 2, lower] = total(2, 1).astype(BF16)
        copies.start(tag + "h-", (half_out, r // 2, lower), (half_in, r, lower), minus)
        full_out[r // 2, 0, lower] = total(1, 1).astype(BF16)
        copies.start(tag + "f+1", (full_out, r // 2, 0, lower), (full_in, r, 0, lower), plus)
        full_out[r // 2, 1, upper] = total(3, 0).astype(BF16)
        copies.start(tag + "f-0", (full_out, r // 2, 1, upper), (full_in, r, 1, upper), minus)

    def ring_own(acc, a, other):
        for step, p in ((1, 0), (3, 1), (0, 0), (0, 1)):
            at = slot_half(step, p)
            acc[a, at] += sib_in[other, at].astype(F32)

    def ring_middle(tag, axis, r, acc, a):
        copies.wait(tag + "h+")
        full_out[r // 2, 0, upper] = (acc[a, slot_half(1, 0)] + half_in[r, upper].astype(F32)).astype(BF16)
        copies.start(tag + "f+0", (full_out, r // 2, 0, upper), (full_in, r, 0, upper), here.along(axis, 1))
        copies.wait(tag + "h-")
        full_out[r // 2, 1, lower] = (acc[a, slot_half(3, 1)] + half_in[r, lower].astype(F32)).astype(BF16)
        copies.start(tag + "f-1", (full_out, r // 2, 1, lower), (full_in, r, 1, lower), here.along(axis, 3))

    def ring_end(tag, r, acc, a):
        copies.wait(tag + "f+0", tag + "f+1", tag + "f-0", tag + "f-1")
        return acc[a, slot(0)] + full_in[r, 0].astype(F32) + full_in[r, 1].astype(F32)

    def hop(which, *parts):
        for p in parts:
            at = pl.ds(p * half, half)
            copies.start(f"hop{which}{p}", (hop_out, which, at), (hop_in, which, at), far_device[which])

    def step(t, carry):
        @pl.when(t == 1)
        def _():
            pass_plus("gx", "x", fine_all, 2)
            pass_minus("gx", "x", fine_all, 2)
            copies.wait("z10", "z11")
            send_both("dy", "y", rows_keep, 1, (0, 1), (1, 0))
            copies.wait("fs", "fx+s", "fx-s", "fx2s")

        @pl.when(t == 2)
        def _():
            sib_near("gx", 2)
            far_coarse(0)
            sib_far("gx", 2)
            pass_plus("dy", "y", rows_keep, 1)
            pass_minus("dy", "y", rows_keep, 1)

        @pl.when(t == 3)
        def _():
            copies.wait("gs", "gx+s", "gx-s", "gx2s", "dy+1", "dy-0")
            far_coarse(-1)
            far_coarse(1)

        @pl.when(t == 4)
        def _():
            ring_start("c0", "y", 3, coarse_acc, 0, None)
            copies.wait("dy++", "dy--")
            far_coarse(2)

        @pl.when(t == 5)
        def _():
            to_sibling(1)

        @pl.when(t == 6)
        def _():
            copies.wait("sum_s1")
            ring_start("f1", "x", 1, fine_acc, 2, 1)
            ring_own(fine_acc, 2, 1)
            ring_middle("c0", "y", 3, coarse_acc, 0)

        @pl.when(t == 7)
        def _():
            to_sibling(0)
            ring_middle("f1", "x", 1, fine_acc, 2)

        late = t // 4
        tile(t + late * (7 - 2 * t), late)
        return carry

    lax.fori_loop(0, 8, step, 0)

    def back(value, unit, inv):
        inner = jnp.sum(unit * value, axis=-1, keepdims=True)
        return ((inv * h) * (value - unit * inner)).astype(BF16)

    def keep(which, start, value_at, buf, a, first):
        n = 32
        for i in range(0, rows, n):
            at = pl.ds(start + i, n)
            dp = back(value_at(i, n), buf[a, pl.ds(first + i, n)].astype(F32), inv_keep[which, at])
            for side in (0, 1):
                dp_keep[which, side, at] = dp[:, side * wide : (side + 1) * wide]

    def grad_to_out(which, start, value, out):
        dp = back(value, unit_keep[which], inv_keep[which, pl.ds(start, rows)])
        fine_acc[2 * which + 1, slot(0)] = dot(dp, heads_in[which], NT)
        return pltpu.make_async_copy(fine_acc.at[2 * which + 1, slot(0)], out, local_sem.at[which])

    core = here.core
    other = 1 - core

    ring_start("c1", "y", 2, coarse_acc, 1, None)
    copies.wait("sum_s0")
    for i in range(4):
        fine_acc[0, slot(i)] += sib_in[0, slot(i)].astype(F32)
    ring_start("f0", "x", 0, fine_acc, 0, None)
    own_sum[1] += ring_end("c0", 3, coarse_acc, 0)
    keep(1, far_rows, lambda i, n: own_sum[1, pl.ds(i, n)], coarse_all, 0, 0)
    keep(1, 0, lambda i, n: coarse_acc[1, pl.ds(i, n)], coarse_all, 1, 0)
    keep(1, rows, lambda i, n: coarse_acc[1, pl.ds(rows + i, n)], coarse_all, 1, rows)
    keep(1, 2 * rows, lambda i, n: coarse_acc[1, pl.ds(2 * rows + i, n)], coarse_all, 1, 2 * rows)
    keep(1, 3 * rows, lambda i, n: coarse_acc[1, pl.ds(3 * rows + i, n)], coarse_all, 1, 3 * rows)
    value = ring_end("f1", 1, fine_acc, 2)
    hop_out[0] = value.astype(BF16)
    fine_acc[2, slot(0)] = value
    hop(0, 0, 1)
    share_out[1] = dot(rows_keep[1], dp_keep[1, other], TN).astype(BF16)
    keep(0, 0, lambda i, n: fine_acc[0, pl.ds(i, n)] + own_sum[0, pl.ds(i, n)], fine_all, 0, 0)
    keep(0, rows, lambda i, n: fine_acc[0, pl.ds(rows + i, n)], fine_all, 0, rows)
    keep(0, 2 * rows, lambda i, n: fine_acc[0, pl.ds(2 * rows + i, n)], fine_all, 0, 2 * rows)
    keep(0, 3 * rows, lambda i, n: fine_acc[0, pl.ds(3 * rows + i, n)], fine_all, 0, 3 * rows)
    copies.start("part_s1", (share_out, 1), (share_in, 1), here.sibling)
    ring_middle("c1", "y", 2, coarse_acc, 1)
    keep(0, far_rows, lambda i, n: fine_acc[2, pl.ds(i, n)], fine_all, 2, 0)
    share_out[0] = dot(rows_keep[0], dp_keep[0, other], TN).astype(BF16)
    copies.start("part_s0", (share_out, 0), (share_in, 0), here.sibling)

    loss = loss_acc[:, 0:128]
    for i in range(1, width // 128):
        loss = loss + loss_acc[:, i * 128 : (i + 1) * 128]
    at_origin = (lax.broadcasted_iota(jnp.int32, (8, 128), 0) + lax.broadcasted_iota(jnp.int32, (8, 128), 1)) == 0
    loss = loss - jnp.where(at_origin, diagonal, 0.0)
    loss_parts[0, 0] = loss
    copies.start("loss_s", (loss_parts, 0, 0), (loss_parts, 0, 1), here.sibling)

    def loss_round(r, axis, place):
        if r == 1:
            copies.wait("loss_s")
            value = loss_parts[0, 0] + loss_parts[0, 1]
        else:
            copies.wait(*[f"loss{r - 1}{d}" for d in (1, 2, 3)])
            q = loss_parts
            value = (q[r - 1, 0] + q[r - 1, 1]) + (q[r - 1, 2] + q[r - 1, 3])
        if axis is None:
            return value
        loss_parts[r, place] = value
        for d in (1, 2, 3):
            copies.start(f"loss{r}{d}", (loss_parts, r, place), (loss_parts, r, place), here.along(axis, d))

    place = {"x": here.x, "y": here.y, "z": here.z}
    n = rows // 4
    for which in (1, 0):
        value = dot(rows_keep[which], dp_keep[which, core], TN)
        copies.wait(f"part_s{which}")
        value = value + share_in[which].astype(F32)
        for q in range(3):
            for j in range(4):
                part_out[q, j, which] = value[j * rows : (j + 1) * rows, q * 128 : (q + 1) * 128].astype(BF16)
    for d in (1, 3, 2):
        for q, (first, _, _) in enumerate(ORDERS):
            copies.start(f"part{q}{d}", (part_out, q, (place[first] + d) % 4), (part_in, q, d - 1), here.along(first, d))

    loss_round(1, "x", here.x)

    for q, (first, second, _) in enumerate(ORDERS):
        copies.wait(*[f"part{q}{d}" for d in (1, 2, 3)])
        value = part_out[q, place[first]].astype(F32)
        for d in range(3):
            value = value + part_in[q, d].astype(F32)
        for j in range(4):
            quarter_out[q, j] = value[:, j * n : (j + 1) * n].astype(BF16)
        for d in (1, 3, 2):
            copies.start(f"quarter{q}{d}", (quarter_out, q, (place[second] + d) % 4), (quarter_in, q, d - 1), here.along(second, d))
    loss_round(2, "y", here.y)
    hop_out[1] = ring_end("c1", 2, coarse_acc, 1).astype(BF16)
    hop(1, 0)
    ring_middle("f0", "x", 0, fine_acc, 0)
    for q, (_, second, third) in enumerate(ORDERS):
        copies.wait(*[f"quarter{q}{d}" for d in (1, 2, 3)])
        value = quarter_out[q, place[second]].astype(F32)
        for d in range(3):
            value = value + quarter_in[q, d].astype(F32)
        column[q, place[third]] = value.astype(BF16)
        mine = (column, q, place[third])
        for d in (1, 3, 2):
            copies.start(f"column{q}{d}", mine, mine, here.along(third, d))
    hop(1, 1)
    loss_round(3, "z", here.z)
    for q, (first, second, third) in enumerate(ORDERS):
        copies.wait(*[f"column{q}{d}" for d in (1, 2, 3)])
        value = column[q, 0].astype(F32)
        for i in range(1, 4):
            value = value + column[q, i].astype(F32)
        heads[core, q, place[first], place[second]] = value.astype(BF16)
        mine = (heads, core, q, place[first], place[second])
        for d in (1, 3, 2):
            copies.start(f"back{q}{d}", mine, mine, here.along(second, d))
    own_sum[0] += ring_end("f0", 0, fine_acc, 0)
    copies.wait("hop00", "hop01")
    fine_copy = grad_to_out(0, 0, own_sum[0] + hop_in[0].astype(F32), fine_grad_out)
    fine_copy.start()
    for q, (first, second, _) in enumerate(ORDERS):
        copies.wait(*[f"back{q}{d}" for d in (1, 2, 3)])
        mine = (heads, core, q, place[first])
        for d in (1, 3, 2):
            copies.start(f"spread{q}{d}", mine, mine, here.along(first, d))
    for q, (first, _, _) in enumerate(ORDERS):
        mine = (heads, core, q, place[first])
        copies.start(f"share{q}0", mine, mine, here.sibling)
    copies.wait("hop10", "hop11")
    coarse_copy = grad_to_out(1, far_rows, own_sum[1] + hop_in[1].astype(F32), coarse_grad_out)
    coarse_copy.start()
    loss_out[...] = loss_round(4, None, None)
    mine_copy = pltpu.make_async_copy(heads.at[core], heads_out.at[core], local_sem.at[2])
    for d in (1, 3, 2):
        for q, (first, _, _) in enumerate(ORDERS):
            copies.wait(f"spread{q}{d}")
            got = (heads, core, q, (place[first] + 4 - d) % 4)
            copies.start(f"share{q}{d}", got, got, here.sibling)
    mine_copy.start()
    copies.wait(*[f"share{q}{d}" for q in range(3) for d in range(4)])
    other_copy = pltpu.make_async_copy(heads.at[other], heads_out.at[other], local_sem.at[3])
    other_copy.start()
    copies.finish()
    fine_copy.wait()
    coarse_copy.wait()
    mine_copy.wait()
    other_copy.wait()


def place_results(pairs, loss_in, fine_in, coarse_in, heads, loss, fine_grad, coarse_grad, fine_head_grad, coarse_head_grad):
    loss[0] = jnp.sum(loss_in[...]) * (1.0 / pairs)
    fine_grad[...] = fine_in[...]
    coarse_grad[...] = coarse_in[...]
    halves, parts, bands, pieces, _, n, lanes = heads.shape
    for side in range(halves):
        for q in range(parts):
            cols = pl.ds((side * parts + q) * lanes, lanes)
            for k in range(bands):
                for j in range(pieces):
                    at = pl.ds((k * pieces + j) * n, n)
                    fine_head_grad[at, cols] = heads[side, q, k, j, 0].astype(F32)
                    coarse_head_grad[at, cols] = heads[side, q, k, j, 1].astype(F32)


def shards(fine_rows, coarse_rows, fine_head, coarse_head, log_scale, bias):
    rows, width = fine_rows.shape
    wide, n = width // 2, rows // 4
    vmem = pl.BlockSpec(memory_space=pltpu.VMEM)
    smem = pl.BlockSpec(memory_space=pltpu.SMEM)
    anywhere = pl.BlockSpec(memory_space=pl.ANY)
    scratch = [
        VMEM((4, 4 * rows, width), BF16),
        VMEM((2, 4 * rows, width), BF16),
        VMEM((4, 4 * rows, width), F32),
        VMEM((2, 4 * rows, width), F32),
        VMEM((2, rows, width), F32),
        VMEM((2, 5 * rows, 1), F32),
        VMEM((2, 5 * rows, width), BF16),
        VMEM((2, width, width), BF16),
        VMEM((2, 8, width), F32),
        VMEM((8, width), F32),
        VMEM((4 * rows, width), BF16),
        VMEM((2, 4 * rows, width), BF16),
        VMEM((2, rows, width), BF16),
        VMEM((4, rows, width), BF16),
        VMEM((2, 2, rows, width), BF16),
        VMEM((4, 2, rows, width), BF16),
        VMEM((2, rows, width), BF16),
        VMEM((2, rows, width), BF16),
        VMEM((2, rows, width), F32),
        VMEM((2, 2, 5 * rows, wide), BF16),
        VMEM((2, width, wide), BF16),
        VMEM((2, width, wide), BF16),
        VMEM((3, 4, 2, rows, 128), BF16),
        VMEM((3, 3, 2, rows, 128), BF16),
        VMEM((3, 4, 2, n, 128), BF16),
        VMEM((3, 3, 2, n, 128), BF16),
        VMEM((3, 4, 2, n, 128), BF16),
        VMEM((2, 3, 4, 4, 2, n, 128), BF16),
        VMEM((4, 4, 8, 128), F32),
        pltpu.SemaphoreType.DMA((N_COPIES,)),
        pltpu.SemaphoreType.DMA((N_COPIES,)),
        pltpu.SemaphoreType.DMA((8,)),
    ]
    tokens = rows * lax.axis_size("grp") * lax.axis_size("mem")
    pair_flops = 6 * (16 * rows) * (8 * rows) * width
    grad = jax.ShapeDtypeStruct((rows, width), F32)
    head = jax.ShapeDtypeStruct((width, width), F32)
    loss, fine_grad, coarse_grad, heads = pl.pallas_call(
        kernel,
        out_shape=(
            jax.ShapeDtypeStruct((8, 128), F32),
            grad,
            grad,
            jax.ShapeDtypeStruct((2, 3, 4, 4, 2, n, 128), BF16),
        ),
        in_specs=[anywhere, anywhere, anywhere, anywhere, smem, smem],
        out_specs=(vmem, anywhere, anywhere, anywhere),
        scratch_shapes=scratch,
        cost_estimate=pl.CostEstimate(flops=pair_flops, bytes_accessed=tokens * width, transcendentals=0),
        compiler_params=pltpu.CompilerParams(collective_id=0, has_side_effects=True, vmem_limit_bytes=60 * 2**20),
    )(fine_rows, coarse_rows, fine_head, coarse_head, log_scale, bias)

    def place(*refs):
        place_results(float(tokens) ** 2, *refs)

    by_rows = pl.BlockSpec((rows * 4, width), lambda i: (i, 0))
    by_halves = pl.BlockSpec((rows, width), lambda i: (i, 0))
    return pl.pallas_call(
        place,
        grid=(1,),
        out_shape=(jax.ShapeDtypeStruct((1,), F32), grad, grad, head, head),
        in_specs=[
            pl.BlockSpec((8, 128), lambda i: (0, 0)),
            by_halves,
            by_halves,
            pl.BlockSpec((2, 3, 4, 4, 2, n, 128), lambda i: (0, 0, i, 0, 0, 0, 0)),
        ],
        out_specs=(smem, by_halves, by_halves, by_rows, by_rows),
    )(loss, fine_grad, coarse_grad, heads)


def solution(mesh):
    placed = (P(("grp", "mem"), None), P(("grp", "mem"), None), P(), P(), P(), P())
    return jax.shard_map(
        shards,
        mesh=mesh,
        in_specs=placed,
        out_specs=(P(), P(("grp", "mem"), None), P(("grp", "mem"), None), P(), P()),
        check_vma=False,
    )
```

```python
import jax
import jax.numpy as jnp
from jax import lax
from jax.experimental import pallas as pl
from jax.experimental.pallas import tpu as pltpu
from jax.sharding import PartitionSpec as P

MESH = pl.DeviceIdType.MESH
EPS = 1e-06
F32 = jnp.float32
BF16 = jnp.bfloat16
VMEM = pltpu.VMEM


def dot(a, b, dims):
    return lax.dot_general(a, b, (dims, ((), ())), preferred_element_type=F32)


NN = ((1,), (0,))
NT = ((1,), (1,))
TN = ((0,), (0,))


class Place:
    def __init__(self):
        grp, mem = lax.axis_index("grp"), lax.axis_index("mem")
        self.core = mem % 2
        self.x, self.y = (mem // 2) % 4, grp % 4
        self.z = (mem // 8) * 2 + grp // 4
        self.steps = {("x", d): self.at(dx=d) for d in (1, 2, 3)}
        self.steps |= {("y", d): self.at(dy=d) for d in (1, 2, 3)}
        self.steps |= {("z", d): self.at(z=(self.z + d) % 4) for d in (1, 2, 3)}
        self.sibling = self.at(core=1 - self.core)
        self.other_hi = self.steps["z", 2]
        self.other_lo = self.at(z=self.z + 1 - 2 * (self.z % 2))

    def at(self, dx=0, dy=0, z=None, core=None):
        x, y = (self.x + dx) % 4, (self.y + dy) % 4
        z = self.z if z is None else z
        core = self.core if core is None else core
        return ((z % 2) * 4 + y, (z // 2) * 8 + x * 2 + core)

    def along(self, axis, step):
        return self.steps[axis, step]


def view(ref, *index):
    return ref.at[index] if index else ref


class Copies:
    def __init__(self, send_sem, recv_sem):
        self.send_sem, self.recv_sem = send_sem, recv_sem
        self.made, self.sent = {}, set()

    def start(self, name, src, dst, device):
        index = len(self.made)
        assert name not in self.made and index < N_COPIES

        def make():
            return pltpu.make_async_remote_copy(
                src_ref=view(*src),
                dst_ref=view(*dst),
                send_sem=self.send_sem.at[index],
                recv_sem=self.recv_sem.at[index],
                device_id=device,
                device_id_type=MESH,
            )

        self.made[name] = make
        make().start()

    def wait(self, *names):
        for name in names:
            self.made[name]().wait_recv()

    def leave(self, *names):
        for name in names:
            self.sent.add(name)
            self.made[name]().wait_send()

    def finish(self):
        self.leave(*[name for name in self.made if name not in self.sent])


N_COPIES = 144
ORDERS = (("x", "y", "z"), ("y", "z", "x"), ("z", "x", "y"))


def kernel(
    fine_rows,
    coarse_rows,
    fine_head,
    coarse_head,
    log_scale,
    bias,
    loss_out,
    fine_grad_out,
    coarse_grad_out,
    heads_out,
    fine_all,
    coarse_all,
    fine_acc,
    coarse_acc,
    unit_keep,
    inv_keep,
    rows_keep,
    heads_in,
    consts,
    loss_acc,
    sib_out,
    sib_in,
    half_out,
    half_in,
    full_out,
    full_in,
    hop_out,
    hop_in,
    own_sum,
    dp_keep,
    share_out,
    share_in,
    part_out,
    part_in,
    quarter_out,
    quarter_in,
    column,
    heads,
    loss_parts,
    send_sem,
    recv_sem,
    local_sem,
):
    rows, width = fine_rows.shape
    half = rows // 2
    wide = width // 2
    here = Place()
    copies = Copies(send_sem, recv_sem)
    upper, lower = pl.ds(0, half), pl.ds(half, half)

    def slot(step):
        return pl.ds((step % 4) * rows, rows)

    def slot_half(step, which):
        return pl.ds((step % 4) * rows + which * half, half)

    barrier = pltpu.get_barrier_semaphore()
    partners = [here.sibling]
    partners += [here.along(axis, step) for axis in "xyz" for step in (1, 2, 3)]
    for device in partners:
        pl.semaphore_signal(barrier, inc=1, device_id=device, device_id_type=MESH)

    loads = [
        pltpu.make_async_copy(fine_rows, rows_keep.at[0, slot(0)], local_sem.at[4]),
        pltpu.make_async_copy(coarse_rows, rows_keep.at[1, pl.ds(4 * rows, rows)], local_sem.at[5]),
        pltpu.make_async_copy(coarse_head, heads_in.at[1], local_sem.at[6]),
        pltpu.make_async_copy(fine_head, heads_in.at[0], local_sem.at[7]),
    ]
    for load in loads:
        load.start()

    consts[0] = 0.5 * jnp.exp(jnp.full((8, width), log_scale[0], F32))
    consts[1] = jnp.full((8, width), 0.5 * bias[0], F32)
    h, shift = consts[0, 0:1, :], consts[1, 0:1, :]

    far_rows = 4 * rows

    def embed(which, start, keep_unit=False):
        at = pl.ds(start, rows)
        proj = dot(rows_keep[which, at], heads_in[which], NN)
        inv = lax.rsqrt(jnp.sum(proj * proj, axis=-1, keepdims=True) + EPS)
        unit = proj * inv
        if keep_unit:
            unit_keep[which] = unit
        inv_keep[which, at] = inv
        return unit.astype(BF16)

    for i in (0, 1):
        loads[i].wait()
    pl.semaphore_wait(barrier, len(partners))
    far_device = (here.other_hi, here.other_lo)

    def to_far(which, start, end):
        for p in (0, 1):
            copies.start(
                f"z{which}{p}",
                (rows_keep, which, pl.ds(start + p * half, half)),
                (rows_keep, which, pl.ds(end + p * half, half)),
                far_device[which],
            )

    def send_both(tag, axis, buf, at, order_plus, order_minus):
        for p in order_plus:
            copies.start(f"{tag}+{p}", (buf, at, slot_half(0, p)), (buf, at, slot_half(-1, p)), here.along(axis, 1))
        for p in order_minus:
            copies.start(f"{tag}-{p}", (buf, at, slot_half(0, p)), (buf, at, slot_half(1, p)), here.along(axis, 3))

    def pass_plus(tag, axis, buf, at):
        copies.wait(tag + "+0")
        copies.start(tag + "++", (buf, at, slot_half(-1, 0)), (buf, at, slot_half(2, 0)), here.along(axis, 1))

    def pass_minus(tag, axis, buf, at):
        copies.wait(tag + "-1")
        copies.start(tag + "--", (buf, at, slot_half(1, 1)), (buf, at, slot_half(2, 1)), here.along(axis, 3))

    def sib_near(tag, at):
        copies.wait(tag + "+1")
        copies.start(tag + "+s", (fine_all, at, slot(-1)), (fine_all, at + 1, slot(-1)), here.sibling)
        copies.wait(tag + "-0")
        copies.start(tag + "-s", (fine_all, at, slot(1)), (fine_all, at + 1, slot(1)), here.sibling)

    def sib_far(tag, at):
        copies.wait(tag + "++", tag + "--")
        copies.start(tag + "2s", (fine_all, at, slot(2)), (fine_all, at + 1, slot(2)), here.sibling)

    to_far(0, 0, far_rows)
    send_both("fx", "x", rows_keep, 0, (0, 1), (1, 0))
    to_far(1, far_rows, 0)
    loads[2].wait()
    coarse_all[0, slot(0)] = embed(1, far_rows, True)
    send_both("cy", "y", coarse_all, 0, (0, 1), (1, 0))
    loads[3].wait()
    fine_all[0, slot(0)] = embed(0, 0, True)
    copies.start("fs", (fine_all, 0, slot(0)), (fine_all, 1, slot(0)), here.sibling)

    coarse_acc[...] = jnp.zeros_like(coarse_acc)
    fine_acc[...] = jnp.zeros_like(fine_acc)
    loss_acc[...] = jnp.zeros_like(loss_acc)

    fine_emb = fine_all[0, slot(0)].astype(F32)
    coarse_emb = coarse_all[0, slot(0)].astype(F32)
    arg = jnp.sum(fine_emb * coarse_emb, axis=-1, keepdims=True) * consts[0, 0:1, 0:1] + consts[1, 0:1, 0:1]
    tanh = jnp.tanh(arg)
    delta = (tanh - 1.0).astype(BF16).astype(F32) - (1.0 + tanh).astype(BF16).astype(F32)
    own_sum[0] = delta * coarse_emb
    own_sum[1] = delta * fine_emb
    diagonal = jnp.sum(2.0 * arg, axis=0, keepdims=True)

    pass_plus("fx", "x", rows_keep, 0)
    pass_minus("fx", "x", rows_keep, 0)
    pass_plus("cy", "y", coarse_all, 0)
    pass_minus("cy", "y", coarse_all, 0)

    def near_fine(step, name):
        fine_all[0, slot(step)] = embed(0, (step % 4) * rows)
        copies.start(name, (fine_all, 0, slot(step)), (fine_all, 1, slot(step)), here.sibling)

    copies.wait("z00", "z01")
    fine_all[2, slot(0)] = embed(0, far_rows)
    send_both("gx", "x", fine_all, 2, (0, 1), (1, 0))
    copies.wait("fx+1")
    near_fine(-1, "fx+s")
    copies.wait("fx-0")
    near_fine(1, "fx-s")
    copies.start("gs", (fine_all, 2, slot(0)), (fine_all, 3, slot(0)), here.sibling)
    copies.wait("fx++", "fx--")
    near_fine(2, "fx2s")
    copies.wait("cy+1", "cy-0", "cy++", "cy--")

    def far_coarse(step):
        coarse_all[1, slot(step)] = embed(1, (step % 4) * rows)

    def tile(fg, cg):
        cols = coarse_all[cg]
        n = 2 * rows
        coefs = []
        for j in range(4 * rows // n):
            at = pl.ds(j * n, n)
            t = jnp.tanh(dot(fine_all[fg, at], cols, NT) * h + shift)
            coef = (1.0 + t).astype(BF16)
            rest = 1.0 - t
            eighth = n // 8
            p = [rest[i * eighth : (i + 1) * eighth] for i in range(8)]
            p = ((p[0] * p[1]) * (p[2] * p[3])) * ((p[4] * p[5]) * (p[6] * p[7]))
            p = jnp.log(p * (1.0 / 256.0))
            for i in range(0, eighth, 8):
                loss_acc[...] -= p[i : i + 8]
            fine_acc[fg, at] += dot(coef, cols, NN)
            coefs.append(coef)
        coarse_acc[cg] += dot(jnp.concatenate(coefs, 0), fine_all[fg], TN)

    def to_sibling(k):
        if k == 0:
            copies.leave("sum_s1")
        sib_out[...] = fine_acc[2 * k + 1].astype(BF16)
        copies.start(f"sum_s{k}", (sib_out,), (sib_in, k), here.sibling)

    def ring_start(tag, axis, r, acc, a, other):
        def total(step, p):
            value = acc[a, slot_half(step, p)]
            return value if other is None else value + sib_in[other, slot_half(step, p)].astype(F32)

        if r % 2 == 0:
            earlier = {0: "f1", 2: "c0"}[r]
            copies.leave(*[earlier + name for name in ("h+", "h-", "f+0", "f+1", "f-0", "f-1")])
        plus, minus = here.along(axis, 1), here.along(axis, 3)
        half_out[r // 2, upper] = total(2, 0).astype(BF16)
        copies.start(tag + "h+", (half_out, r // 2, upper), (half_in, r, upper), plus)
        half_out[r // 2, lower] = total(2, 1).astype(BF16)
        copies.start(tag + "h-", (half_out, r // 2, lower), (half_in, r, lower), minus)
        full_out[r // 2, 0, lower] = total(1, 1).astype(BF16)
        copies.start(tag + "f+1", (full_out, r // 2, 0, lower), (full_in, r, 0, lower), plus)
        full_out[r // 2, 1, upper] = total(3, 0).astype(BF16)
        copies.start(tag + "f-0", (full_out, r // 2, 1, upper), (full_in, r, 1, upper), minus)

    def ring_own(acc, a, other):
        for step, p in ((1, 0), (3, 1), (0, 0), (0, 1)):
            at = slot_half(step, p)
            acc[a, at] += sib_in[other, at].astype(F32)

    def ring_middle(tag, axis, r, acc, a):
        copies.wait(tag + "h+")
        full_out[r // 2, 0, upper] = (acc[a, slot_half(1, 0)] + half_in[r, upper].astype(F32)).astype(BF16)
        copies.start(tag + "f+0", (full_out, r // 2, 0, upper), (full_in, r, 0, upper), here.along(axis, 1))
        copies.wait(tag + "h-")
        full_out[r // 2, 1, lower] = (acc[a, slot_half(3, 1)] + half_in[r, lower].astype(F32)).astype(BF16)
        copies.start(tag + "f-1", (full_out, r // 2, 1, lower), (full_in, r, 1, lower), here.along(axis, 3))

    def ring_end(tag, r, acc, a):
        copies.wait(tag + "f+0", tag + "f+1", tag + "f-0", tag + "f-1")
        return acc[a, slot(0)] + full_in[r, 0].astype(F32) + full_in[r, 1].astype(F32)

    def hop(which, *parts):
        for p in parts:
            at = pl.ds(p * half, half)
            copies.start(f"hop{which}{p}", (hop_out, which, at), (hop_in, which, at), far_device[which])

    def step(t, carry):
        @pl.when(t == 1)
        def _():
            pass_plus("gx", "x", fine_all, 2)
            pass_minus("gx", "x", fine_all, 2)
            copies.wait("z10", "z11")
            send_both("dy", "y", rows_keep, 1, (0, 1), (1, 0))
            copies.wait("fs", "fx+s", "fx-s", "fx2s")

        @pl.when(t == 2)
        def _():
            sib_near("gx", 2)
            far_coarse(0)
            sib_far("gx", 2)
            pass_plus("dy", "y", rows_keep, 1)
            pass_minus("dy", "y", rows_keep, 1)

        @pl.when(t == 3)
        def _():
            copies.wait("gs", "gx+s", "gx-s", "gx2s", "dy+1", "dy-0")
            far_coarse(-1)
            far_coarse(1)

        @pl.when(t == 4)
        def _():
            ring_start("c0", "y", 3, coarse_acc, 0, None)
            copies.wait("dy++", "dy--")
            far_coarse(2)

        @pl.when(t == 5)
        def _():
            to_sibling(1)

        @pl.when(t == 6)
        def _():
            copies.wait("sum_s1")
            ring_start("f1", "x", 1, fine_acc, 2, 1)
            ring_own(fine_acc, 2, 1)
            ring_middle("c0", "y", 3, coarse_acc, 0)

        @pl.when(t == 7)
        def _():
            to_sibling(0)
            ring_middle("f1", "x", 1, fine_acc, 2)

        late = t // 4
        tile(t + late * (7 - 2 * t), late)
        return carry

    lax.fori_loop(0, 8, step, 0)

    def back(value, unit, inv):
        inner = jnp.sum(unit * value, axis=-1, keepdims=True)
        return ((inv * h) * (value - unit * inner)).astype(BF16)

    def keep(which, start, value_at, buf, a, first):
        n = 32
        for i in range(0, rows, n):
            at = pl.ds(start + i, n)
            dp = back(value_at(i, n), buf[a, pl.ds(first + i, n)].astype(F32), inv_keep[which, at])
            for side in (0, 1):
                dp_keep[which, side, at] = dp[:, side * wide : (side + 1) * wide]

    def grad_to_out(which, start, value, out):
        dp = back(value, unit_keep[which], inv_keep[which, pl.ds(start, rows)])
        fine_acc[2 * which + 1, slot(0)] = dot(dp, heads_in[which], NT)
        return pltpu.make_async_copy(fine_acc.at[2 * which + 1, slot(0)], out, local_sem.at[which])

    core = here.core
    other = 1 - core

    ring_start("c1", "y", 2, coarse_acc, 1, None)
    copies.wait("sum_s0")
    for i in range(4):
        fine_acc[0, slot(i)] += sib_in[0, slot(i)].astype(F32)
    ring_start("f0", "x", 0, fine_acc, 0, None)
    own_sum[1] += ring_end("c0", 3, coarse_acc, 0)
    keep(1, far_rows, lambda i, n: own_sum[1, pl.ds(i, n)], coarse_all, 0, 0)
    keep(1, 0, lambda i, n: coarse_acc[1, pl.ds(i, n)], coarse_all, 1, 0)
    keep(1, rows, lambda i, n: coarse_acc[1, pl.ds(rows + i, n)], coarse_all, 1, rows)
    keep(1, 2 * rows, lambda i, n: coarse_acc[1, pl.ds(2 * rows + i, n)], coarse_all, 1, 2 * rows)
    keep(1, 3 * rows, lambda i, n: coarse_acc[1, pl.ds(3 * rows + i, n)], coarse_all, 1, 3 * rows)
    value = ring_end("f1", 1, fine_acc, 2)
    hop_out[0] = value.astype(BF16)
    fine_acc[2, slot(0)] = value
    hop(0, 0)
    share_out[1] = dot(rows_keep[1], dp_keep[1, other], TN).astype(BF16)
    keep(0, 0, lambda i, n: fine_acc[0, pl.ds(i, n)] + own_sum[0, pl.ds(i, n)], fine_all, 0, 0)
    keep(0, rows, lambda i, n: fine_acc[0, pl.ds(rows + i, n)], fine_all, 0, rows)
    keep(0, 2 * rows, lambda i, n: fine_acc[0, pl.ds(2 * rows + i, n)], fine_all, 0, 2 * rows)
    keep(0, 3 * rows, lambda i, n: fine_acc[0, pl.ds(3 * rows + i, n)], fine_all, 0, 3 * rows)
    copies.start("part_s1", (share_out, 1), (share_in, 1), here.sibling)
    ring_middle("c1", "y", 2, coarse_acc, 1)
    keep(0, far_rows, lambda i, n: fine_acc[2, pl.ds(i, n)], fine_all, 2, 0)
    share_out[0] = dot(rows_keep[0], dp_keep[0, other], TN).astype(BF16)
    copies.start("part_s0", (share_out, 0), (share_in, 0), here.sibling)

    loss = loss_acc[:, 0:128]
    for i in range(1, width // 128):
        loss = loss + loss_acc[:, i * 128 : (i + 1) * 128]
    at_origin = (lax.broadcasted_iota(jnp.int32, (8, 128), 0) + lax.broadcasted_iota(jnp.int32, (8, 128), 1)) == 0
    loss = loss - jnp.where(at_origin, diagonal, 0.0)
    loss_parts[0, 0] = loss
    copies.start("loss_s", (loss_parts, 0, 0), (loss_parts, 0, 1), here.sibling)

    def loss_round(r, axis, place):
        if r == 1:
            copies.wait("loss_s")
            value = loss_parts[0, 0] + loss_parts[0, 1]
        else:
            copies.wait(*[f"loss{r - 1}{d}" for d in (1, 2, 3)])
            q = loss_parts
            value = (q[r - 1, 0] + q[r - 1, 1]) + (q[r - 1, 2] + q[r - 1, 3])
        if axis is None:
            return value
        loss_parts[r, place] = value
        for d in (1, 2, 3):
            copies.start(f"loss{r}{d}", (loss_parts, r, place), (loss_parts, r, place), here.along(axis, d))

    place = {"x": here.x, "y": here.y, "z": here.z}
    n = rows // 4
    for which in (1, 0):
        value = dot(rows_keep[which], dp_keep[which, core], TN)
        copies.wait(f"part_s{which}")
        value = value + share_in[which].astype(F32)
        for q in range(3):
            for j in range(4):
                part_out[q, j, which] = value[j * rows : (j + 1) * rows, q * 128 : (q + 1) * 128].astype(BF16)
    for d in (1, 3, 2):
        for q, (first, _, _) in enumerate(ORDERS):
            copies.start(f"part{q}{d}", (part_out, q, (place[first] + d) % 4), (part_in, q, d - 1), here.along(first, d))

    loss_round(1, "x", here.x)

    for q, (first, second, _) in enumerate(ORDERS):
        copies.wait(*[f"part{q}{d}" for d in (1, 2, 3)])
        value = part_out[q, place[first]].astype(F32)
        for d in range(3):
            value = value + part_in[q, d].astype(F32)
        for j in range(4):
            quarter_out[q, j] = value[:, j * n : (j + 1) * n].astype(BF16)
        for d in (1, 3, 2):
            copies.start(f"quarter{q}{d}", (quarter_out, q, (place[second] + d) % 4), (quarter_in, q, d - 1), here.along(second, d))
    loss_round(2, "y", here.y)
    hop_out[1] = ring_end("c1", 2, coarse_acc, 1).astype(BF16)
    hop(1, 0)
    ring_middle("f0", "x", 0, fine_acc, 0)
    for q, (_, second, third) in enumerate(ORDERS):
        copies.wait(*[f"quarter{q}{d}" for d in (1, 2, 3)])
        value = quarter_out[q, place[second]].astype(F32)
        for d in range(3):
            value = value + quarter_in[q, d].astype(F32)
        column[q, place[third]] = value.astype(BF16)
        mine = (column, q, place[third])
        for d in (1, 3, 2):
            copies.start(f"column{q}{d}", mine, mine, here.along(third, d))
    hop(1, 1)
    loss_round(3, "z", here.z)
    for q, (first, second, third) in enumerate(ORDERS):
        copies.wait(*[f"column{q}{d}" for d in (1, 2, 3)])
        value = column[q, 0].astype(F32)
        for i in range(1, 4):
            value = value + column[q, i].astype(F32)
        heads[core, q, place[first], place[second]] = value.astype(BF16)
        mine = (heads, core, q, place[first], place[second])
        for d in (1, 3, 2):
            copies.start(f"back{q}{d}", mine, mine, here.along(second, d))
    hop(0, 1)
    for q, (first, second, _) in enumerate(ORDERS):
        copies.wait(*[f"back{q}{d}" for d in (1, 2, 3)])
        mine = (heads, core, q, place[first])
        for d in (1, 3, 2):
            copies.start(f"spread{q}{d}", mine, mine, here.along(first, d))
    for q, (first, _, _) in enumerate(ORDERS):
        mine = (heads, core, q, place[first])
        copies.start(f"share{q}0", mine, mine, here.sibling)
    own_sum[0] += ring_end("f0", 0, fine_acc, 0)
    copies.wait("hop00", "hop01")
    fine_copy = grad_to_out(0, 0, own_sum[0] + hop_in[0].astype(F32), fine_grad_out)
    fine_copy.start()
    copies.wait("hop10", "hop11")
    coarse_copy = grad_to_out(1, far_rows, own_sum[1] + hop_in[1].astype(F32), coarse_grad_out)
    coarse_copy.start()
    loss_out[...] = loss_round(4, None, None)
    mine_copy = pltpu.make_async_copy(heads.at[core], heads_out.at[core], local_sem.at[2])
    for d in (1, 3, 2):
        for q, (first, _, _) in enumerate(ORDERS):
            copies.wait(f"spread{q}{d}")
            got = (heads, core, q, (place[first] + 4 - d) % 4)
            copies.start(f"share{q}{d}", got, got, here.sibling)
    mine_copy.start()
    copies.wait(*[f"share{q}{d}" for q in range(3) for d in range(4)])
    other_copy = pltpu.make_async_copy(heads.at[other], heads_out.at[other], local_sem.at[3])
    other_copy.start()
    copies.finish()
    fine_copy.wait()
    coarse_copy.wait()
    mine_copy.wait()
    other_copy.wait()


def place_results(pairs, loss_in, fine_in, coarse_in, heads, loss, fine_grad, coarse_grad, fine_head_grad, coarse_head_grad):
    loss[0] = jnp.sum(loss_in[...]) * (1.0 / pairs)
    fine_grad[...] = fine_in[...]
    coarse_grad[...] = coarse_in[...]
    halves, parts, bands, pieces, _, n, lanes = heads.shape
    for side in range(halves):
        for q in range(parts):
            cols = pl.ds((side * parts + q) * lanes, lanes)
            for k in range(bands):
                for j in range(pieces):
                    at = pl.ds((k * pieces + j) * n, n)
                    fine_head_grad[at, cols] = heads[side, q, k, j, 0].astype(F32)
                    coarse_head_grad[at, cols] = heads[side, q, k, j, 1].astype(F32)


def shards(fine_rows, coarse_rows, fine_head, coarse_head, log_scale, bias):
    rows, width = fine_rows.shape
    wide, n = width // 2, rows // 4
    vmem = pl.BlockSpec(memory_space=pltpu.VMEM)
    smem = pl.BlockSpec(memory_space=pltpu.SMEM)
    anywhere = pl.BlockSpec(memory_space=pl.ANY)
    scratch = [
        VMEM((4, 4 * rows, width), BF16),
        VMEM((2, 4 * rows, width), BF16),
        VMEM((4, 4 * rows, width), F32),
        VMEM((2, 4 * rows, width), F32),
        VMEM((2, rows, width), F32),
        VMEM((2, 5 * rows, 1), F32),
        VMEM((2, 5 * rows, width), BF16),
        VMEM((2, width, width), BF16),
        VMEM((2, 8, width), F32),
        VMEM((8, width), F32),
        VMEM((4 * rows, width), BF16),
        VMEM((2, 4 * rows, width), BF16),
        VMEM((2, rows, width), BF16),
        VMEM((4, rows, width), BF16),
        VMEM((2, 2, rows, width), BF16),
        VMEM((4, 2, rows, width), BF16),
        VMEM((2, rows, width), BF16),
        VMEM((2, rows, width), BF16),
        VMEM((2, rows, width), F32),
        VMEM((2, 2, 5 * rows, wide), BF16),
        VMEM((2, width, wide), BF16),
        VMEM((2, width, wide), BF16),
        VMEM((3, 4, 2, rows, 128), BF16),
        VMEM((3, 3, 2, rows, 128), BF16),
        VMEM((3, 4, 2, n, 128), BF16),
        VMEM((3, 3, 2, n, 128), BF16),
        VMEM((3, 4, 2, n, 128), BF16),
        VMEM((2, 3, 4, 4, 2, n, 128), BF16),
        VMEM((4, 4, 8, 128), F32),
        pltpu.SemaphoreType.DMA((N_COPIES,)),
        pltpu.SemaphoreType.DMA((N_COPIES,)),
        pltpu.SemaphoreType.DMA((8,)),
    ]
    tokens = rows * lax.axis_size("grp") * lax.axis_size("mem")
    pair_flops = 6 * (16 * rows) * (8 * rows) * width
    grad = jax.ShapeDtypeStruct((rows, width), F32)
    head = jax.ShapeDtypeStruct((width, width), F32)
    loss, fine_grad, coarse_grad, heads = pl.pallas_call(
        kernel,
        out_shape=(
            jax.ShapeDtypeStruct((8, 128), F32),
            grad,
            grad,
            jax.ShapeDtypeStruct((2, 3, 4, 4, 2, n, 128), BF16),
        ),
        in_specs=[anywhere, anywhere, anywhere, anywhere, smem, smem],
        out_specs=(vmem, anywhere, anywhere, anywhere),
        scratch_shapes=scratch,
        cost_estimate=pl.CostEstimate(flops=pair_flops, bytes_accessed=tokens * width, transcendentals=0),
        compiler_params=pltpu.CompilerParams(collective_id=0, has_side_effects=True, vmem_limit_bytes=60 * 2**20),
    )(fine_rows, coarse_rows, fine_head, coarse_head, log_scale, bias)

    def place(*refs):
        place_results(float(tokens) ** 2, *refs)

    by_rows = pl.BlockSpec((rows * 4, width), lambda i: (i, 0))
    by_halves = pl.BlockSpec((rows, width), lambda i: (i, 0))
    return pl.pallas_call(
        place,
        grid=(1,),
        out_shape=(jax.ShapeDtypeStruct((1,), F32), grad, grad, head, head),
        in_specs=[
            pl.BlockSpec((8, 128), lambda i: (0, 0)),
            by_halves,
            by_halves,
            pl.BlockSpec((2, 3, 4, 4, 2, n, 128), lambda i: (0, 0, i, 0, 0, 0, 0)),
        ],
        out_specs=(smem, by_halves, by_halves, by_rows, by_rows),
    )(loss, fine_grad, coarse_grad, heads)


def solution(mesh):
    placed = (P(("grp", "mem"), None), P(("grp", "mem"), None), P(), P(), P(), P())
    return jax.shard_map(
        shards,
        mesh=mesh,
        in_specs=placed,
        out_specs=(P(), P(("grp", "mem"), None), P(("grp", "mem"), None), P(), P()),
        check_vma=False,
    )
```
